512 devices in a mesh: dp: 32 (over x, z_lo), tile: 16 (over z_hi, y, core).
Axes of the slice: x: 4, y: 4, z: 16 (z_hi: 2, z_lo: 8; z = z_hi * 8 + z_lo), core: 2. Of those that a mesh axis runs over, the one named last changes fastest.
Arguments:
- tokens: bfloat16 [32, 16, 16, 16, 384], P('dp', 'tile'), may hold values from -1.5 to 1.5
- timesteps: int32 [32], P('dp'), may hold values from 0 to 999
- cond_weight: bfloat16 [256, 384], replicated, may hold values from -0.375 to 0.375
- qkv_weight: bfloat16 [384, 1152], replicated, may hold values from -0.3125 to 0.3125
- head_scale: float32 [6], replicated, may hold values from 4 to 20
- out_weight: bfloat16 [384, 384], replicated, may hold values from -0.875 to 0.875
- cotangent: bfloat16 [32, 16, 16, 16, 384], P('dp', 'tile'), may hold values from -0.015625 to 0.015625
Outputs:
- updated: bfloat16 [32, 16, 16, 16, 384], P('dp', 'tile')
- grad_out_weight: float32 [384, 384], replicated
The draws below stay inside these ranges and needn't reach their ends.
All inputs are finite; a program needn't handle non-finite values.
Results may differ from the reference program's by a relative error of at most 0.015.
Values may be sent and summed in bfloat16 or wider, within the bound.
A program may use at most 64 MiB of HBM per device.

```python
import math
import jax
import jax.numpy as jnp
from jax import lax

CH = 384
HEADS = 6
EMB = 256
S = 16
TILES = 16
IMAGES = 32


def plant(entries, rng, least, largest):
    longest = entries.shape.index(max(entries.shape))
    spots = []
    for shift in (0, 1):
        where = [jax.random.randint(jax.random.fold_in(rng, axis), (), 0, length) for axis, length in enumerate(entries.shape)]
        where[longest] = (where[longest] + shift) % entries.shape[longest]
        spots.append(tuple(where))
    return entries.at[spots[0]].set(least).at[spots[1]].set(largest)


def steps_of(stream_key, shape, shards, least, high):
    def one(dim, blocks):
        heights = jax.random.uniform(jax.random.fold_in(jax.random.fold_in(stream_key, 6), dim), (blocks,), jnp.float32, least / len(shards), high / len(shards))
        return jnp.repeat(jnp.exp(heights), shape[dim] // blocks).reshape((-1,) + (1,) * (len(shape) - dim - 1))

    factor_of = one(*shards[0])
    for cut in shards[1:]:
        factor_of = factor_of * one(*cut)
    return factor_of


def centred(key, extent, deviation, limit, shards=(), kind=jnp.bfloat16):
    array = jax.random.normal(key, extent, jnp.float32) * deviation
    if len(shards) > 0:
        array = steps_of(key, extent, shards, -0.22, 0.18) * array
    return jnp.clip(array, min=-limit, max=limit).astype(kind)


def setup_inputs(seed: int = 0) -> dict:
    streams_of = jax.random.split(jax.random.key(seed), 8)
    tokens = centred(streams_of[0], (IMAGES, TILES, S, S, CH), 0.25, 1.5, ((0, 32), (1, 16)))
    timesteps = plant(jax.random.randint(streams_of[1], (IMAGES,), 0, 1000), jax.random.fold_in(streams_of[1], 1), 0, 999).astype(jnp.int32)
    cond_weight = centred(streams_of[2], (EMB, CH), EMB ** -0.5, 0.375)
    qkv_weight = centred(streams_of[3], (CH, 3 * CH), CH ** -0.5, 0.3125)
    head_scale = jnp.clip(jnp.exp(jax.random.uniform(streams_of[4], (HEADS,), jnp.float32, math.log(4.0), math.log(20.0))), 4.0, 20.0)
    out_weight = centred(streams_of[5], (CH, CH), (CH // 8) ** -0.5, 0.875)
    cotangent = centred(streams_of[6], (IMAGES, TILES, S, S, CH), (IMAGES * TILES * S * S) ** -0.5, 0.015625, ((0, 32), (1, 16)))
    return dict(tokens=tokens, timesteps=timesteps, cond_weight=cond_weight, qkv_weight=qkv_weight, head_scale=head_scale, out_weight=out_weight, cotangent=cotangent)


def normalize(vectors):
    return vectors / jnp.sqrt(lax.optimization_barrier(jnp.sum(vectors * vectors, axis=-1, keepdims=True)) + 1e-06)

def reference(tokens, timesteps, cond_weight, qkv_weight, head_scale, out_weight, cotangent):
    grid_count = math.isqrt(TILES)
    image_side = grid_count * S
    head_dim = CH // HEADS
    half_count = EMB // 2
    frequency = jnp.exp(-math.log(10000.0) * jnp.arange(half_count, dtype=jnp.float32) / half_count)
    angles = timesteps.astype(jnp.float32)[:, None] * frequency[None, :]
    features = jnp.concatenate([jnp.cos(angles), jnp.sin(angles)], axis=1)
    norm_gains = 1.0 + jnp.dot(features, cond_weight.astype(jnp.float32), precision=lax.Precision.HIGHEST)
    images = tokens.reshape(IMAGES, grid_count, grid_count, S, S, CH).transpose(0, 1, 3, 2, 4, 5).reshape(IMAGES, image_side, image_side, CH)
    cot_images = cotangent.reshape(IMAGES, grid_count, grid_count, S, S, CH).transpose(0, 1, 3, 2, 4, 5).reshape(IMAGES, image_side, image_side, CH)
    inside = jnp.pad(jnp.ones((image_side, image_side), jnp.float32), 3)

    def per_image(grad_sum, image_item):
        image_rows, norm_gain, cot_rows = image_item
        widened = image_rows.astype(jnp.float32)
        mean_square = lax.optimization_barrier(jnp.mean(widened * widened, axis=-1, keepdims=True))
        normed = (widened * lax.rsqrt(mean_square + 1e-06) * norm_gain).astype(jnp.bfloat16)
        projected = jnp.dot(normed.reshape(-1, CH), qkv_weight, preferred_element_type=jnp.float32)
        shaped = (image_side, image_side, HEADS, head_dim)
        query_unit = normalize(projected[:, :CH].reshape(shaped)).astype(jnp.bfloat16)
        key_unit = normalize(projected[:, CH:2 * CH].reshape(shaped)).astype(jnp.bfloat16)
        value_rows = projected[:, 2 * CH:].reshape(shaped).astype(jnp.bfloat16)
        pad_form = ((3, 3), (3, 3), (0, 0), (0, 0))
        key_padded = jnp.pad(key_unit, pad_form).astype(jnp.float32)
        value_padded = jnp.pad(value_rows, pad_form).astype(jnp.float32)
        query_wide = query_unit.astype(jnp.float32)
        expscores = []
        for row_step in range(7):
            for col_step in range(7):
                key_shift = key_padded[row_step:row_step + image_side, col_step:col_step + image_side]
                score = lax.optimization_barrier(jnp.sum(query_wide * key_shift, axis=-1)) * head_scale
                allowed = inside[row_step:row_step + image_side, col_step:col_step + image_side]
                expscores.append(jnp.exp(score) * allowed[:, :, None])
        denominator = sum(expscores)
        attended = jnp.zeros(shaped, jnp.float32)
        offset_number = 0
        for row_step in range(7):
            for col_step in range(7):
                weight = (expscores[offset_number] / denominator).astype(jnp.bfloat16).astype(jnp.float32)
                value_shift = value_padded[row_step:row_step + image_side, col_step:col_step + image_side]
                attended = attended + weight[..., None] * value_shift
                offset_number += 1
        attended = attended.astype(jnp.bfloat16).reshape(-1, CH)
        branch = jnp.dot(attended, out_weight, preferred_element_type=jnp.float32)
        updated = (widened.reshape(-1, CH) + branch).astype(jnp.bfloat16)
        grad_sum = grad_sum + jnp.dot(attended.T, cot_rows.reshape(-1, CH), preferred_element_type=jnp.float32)
        return (grad_sum, updated)
    grad_out_weight, updated = lax.scan(per_image, jnp.zeros((CH, CH), jnp.float32), (images, norm_gains, cot_images))
    updated = updated.reshape(IMAGES, grid_count, S, grid_count, S, CH).transpose(0, 1, 3, 2, 4, 5).reshape(IMAGES, TILES, S, S, CH)
    return (updated, grad_out_weight)
```

```python
import math

import jax
import jax.numpy as jnp
from jax import lax
from jax.experimental import pallas as pl
from jax.experimental.pallas import tpu as pltpu
from jax.sharding import PartitionSpec as P

MESH = pl.DeviceIdType.MESH
F32, BF16 = jnp.float32, jnp.bfloat16
TOKENS = 256
CH = 384
HALO = 256
ROWS = 16
OWNERS = 12
HALF = OWNERS * ROWS
FAR = -16384.0
SENDS = (
    (1, 0, 208, 48, 0),
    (-1, 0, 0, 48, 48),
    (0, 1, 0, 48, 96),
    (0, -1, 48, 48, 144),
    (1, 1, 96, 16, 192),
    (1, -1, 112, 16, 208),
    (-1, 1, 128, 16, 224),
    (-1, -1, 144, 16, 240),
)


def mm(a, b):
    return jnp.dot(a, b, preferred_element_type=F32)


def iota(shape, axis):
    return lax.broadcasted_iota(jnp.int32, shape, axis)


def thirds(m):
    return (m >= 3).astype(jnp.int32) + (m >= 6).astype(jnp.int32) + (m >= 9).astype(jnp.int32)


def pick_matrix():
    r = iota((160, TOKENS), 0)
    m48 = jnp.where(r >= 48, r - 48, r)
    side = (m48 % 16) * 16 + m48 // 16 + jnp.where(r < 48, 13, 0)
    m = r % 16
    third = thirds(m)
    corner = third * 16 + m - 3 * third + jnp.where(r < 128, 13 * 16, 0)
    corner = corner + jnp.where((r < 112) | ((r >= 128) & (r < 144)), 13, 0)
    corner = jnp.where(m < 9, corner, -1)
    wanted = jnp.where(r < 96, side, corner)
    return jnp.where(iota((160, TOKENS), 1) == wanted, 1.0, 0.0).astype(BF16)


def key_marks(kr, kc, known, base):
    f = iota(kr.shape, 1) - base
    apart = jnp.where(f < 16, jnp.abs(kr - f), jnp.abs(kc - (f - 16)))
    bad = (apart > 3) | jnp.logical_not(known)
    return jnp.where(bad & (f >= 0) & (f < 32), FAR, 0.0)


def own_places(shape):
    i = iota(shape, 0)
    return i // 16, i % 16


def halo_places(shape, grid_row, grid_col):
    j = iota(shape, 0)
    m = jnp.where(j >= 144, j - 144, jnp.where(j >= 96, j - 96, jnp.where(j >= 48, j - 48, j)))
    first, second = m // 16, m % 16
    c = j % 16
    third = thirds(c)
    rest = c - 3 * third
    kr = jnp.where(j < 48, first - 3, jnp.where(j < 96, first + 16, second))
    kc = jnp.where(j < 96, second, jnp.where(j < 144, first - 3, first + 16))
    corner = j >= 192
    kr = jnp.where(corner, third + jnp.where(j < 224, -3, 16), kr)
    west = (j < 208) | ((j >= 224) & (j < 240))
    kc = jnp.where(corner, rest + jnp.where(west, -3, 16), kc)
    known = jnp.logical_not(corner & (c >= 9))
    known = known & ((kr >= 0) | (grid_row > 0)) & ((kr < 16) | (grid_row < 3))
    known = known & ((kc >= 0) | (grid_col > 0)) & ((kc < 16) | (grid_col < 3))
    return kr, kc, known


def device(x, y, core, z):
    return (x * 8 + lax.rem(z, 8), (z // 8) * 8 + y * 2 + core)


def owner_of(k, core):
    x, rest = k // 3, lax.rem(k, 3)
    y = rest + jnp.where(rest >= x, 1, 0)
    return x, jnp.where(core == 0, y, 3 - y)


def owned_by(x, y, core):
    y = jnp.where(core == 0, y, 3 - y)
    return jnp.where(x == y, OWNERS, x * 3 + y - jnp.where(y > x, 1, 0))


def kernel(
    tok_hbm, cot_hbm, qkv_hbm, out_w_hbm, cond_hbm, scale_hbm, step_ref,
    upd_ref, grad_ref,
    tok, cot, qkv, out_w, cond, scale_ref, packed, halo, q_s, k_s, v_s, acc, att,
    own, cross, sent, part, z1, z2, gath,
    in_sem, halo_s, halo_r, cross_s, cross_r, s1, r1, sz1, rz1, sz2, rz2, s3, r3, s4, r4,
):
    dp, tile = lax.axis_index("dp"), lax.axis_index("tile")
    grid_row, grid_col = tile // 4, lax.rem(tile, 4)
    x, z = dp // 8, (tile // 8) * 8 + lax.rem(dp, 8)
    y, core = lax.rem(tile, 8) // 2, lax.rem(tile, 2)
    a, b = z // 4, lax.rem(z, 4)
    chip = x * 4 + y
    mine = owned_by(x, y, core)
    owns = mine < OWNERS
    partner = (dp, tile + 1 - 2 * core)

    loads = [
        pltpu.make_async_copy(src, dst, in_sem.at[i])
        for i, (src, dst) in enumerate(((tok_hbm, tok), (cond_hbm, cond), (qkv_hbm, qkv), (cot_hbm, cot), (out_w_hbm, out_w), (scale_hbm, scale_ref)))
    ]
    for load in loads:
        load.start()

    halo[...] = jnp.zeros_like(halo)
    barrier = pltpu.get_barrier_semaphore()

    def there(dr, dc):
        ok = True
        if dr:
            ok = (grid_row < 3) if dr > 0 else (grid_row > 0)
        if dc:
            right = (grid_col < 3) if dc > 0 else (grid_col > 0)
            ok = (ok & right) if dr else right
        return ok

    near = 0
    for dr, dc, _, _, _ in SENDS:
        ok = there(dr, dc)
        near = near + jnp.where(ok, 1, 0)

        @pl.when(ok)
        def _():
            pl.semaphore_signal(barrier, inc=1, device_id=(dp, tile + 4 * dr + dc), device_id_type=MESH)

    pl.semaphore_signal(barrier, inc=1, device_id=partner, device_id_type=MESH)
    for i in range(1, 4):
        pl.semaphore_signal(barrier, inc=1, device_id=device(x, y, core, a * 4 + lax.rem(b + i, 4)), device_id_type=MESH)
        pl.semaphore_signal(barrier, inc=1, device_id=device(x, y, core, lax.rem(a + i, 4) * 4 + b), device_id_type=MESH)

    def greet(i, _):
        c = lax.rem(chip + i, 16)
        pl.semaphore_signal(barrier, inc=1, device_id=device(c // 4, lax.rem(c, 4), core, z), device_id_type=MESH)
        return 0

    lax.fori_loop(1, 16, greet, 0)

    loads[0].wait()
    packed[...] = mm(pick_matrix(), tok[...]).astype(BF16)

    pl.semaphore_wait(barrier, 22 + near)

    def halo_copy(i):
        dr, dc, place, count, into = SENDS[i]
        source = tok if dc == 0 else packed
        return pltpu.make_async_remote_copy(
            src_ref=source.at[pl.ds(place, count)], dst_ref=halo.at[pl.ds(into, count)],
            send_sem=halo_s, recv_sem=halo_r.at[i], device_id=(dp, tile + 4 * dr + dc), device_id_type=MESH,
        )

    for i, (dr, dc, _, _, _) in enumerate(SENDS):
        @pl.when(there(dr, dc))
        def _():
            halo_copy(i).start()

    loads[1].wait()
    loads[5].wait()
    frequency = jnp.exp((-math.log(10000.0) / 128) * iota((8, 128), 1).astype(F32))
    angles = step_ref[0].astype(F32) * frequency
    features = jnp.concatenate([jnp.cos(angles), jnp.sin(angles)], axis=1)
    high = features.astype(BF16)
    rest = features - high.astype(F32)
    middle = rest.astype(BF16)
    low = (rest - middle.astype(F32)).astype(BF16)
    gain = 1.0 + mm(high, cond[...]) + mm(middle, cond[...]) + mm(low, cond[...])
    gain = gain[0:1]

    same_head = jnp.where((iota((128, 128), 0) < 64) == (iota((128, 128), 1) < 64), 1.0, 0.0).astype(BF16)
    same_head = jnp.concatenate([same_head, same_head], axis=0)

    def normed(rows):
        wide = rows.astype(F32)
        mean_square = jnp.mean(wide * wide, axis=-1, keepdims=True)
        return (wide * lax.rsqrt(mean_square + 1e-06) * gain).astype(BF16)

    def unit(vectors):
        square = vectors * vectors
        high = square.astype(BF16)
        low = (square - high.astype(F32)).astype(BF16)
        total = mm(jnp.concatenate([high, low], axis=1), same_head)
        return vectors * lax.rsqrt(total + 1e-06)

    left = iota((TOKENS, 128), 1) < 64

    def put_keys(rows, where, kr, kc, known):
        even, odd = key_marks(kr, kc, known, 64), key_marks(kr, kc, known, 0)
        for p in range(3):
            key = unit(mm(rows, qkv[:, CH + 128 * p:CH + 128 * (p + 1)]))
            k_s[p, 0, where] = jnp.where(left, key, even).astype(BF16)
            k_s[p, 1, where] = jnp.where(left, odd, key).astype(BF16)
            value = mm(rows, qkv[:, 2 * CH + 128 * p:2 * CH + 128 * (p + 1)])
            v_s[p, where, 0:128] = value.astype(BF16)
            v_s[p, where, 128:256] = jnp.ones((TOKENS, 128), BF16)

    def attend(p, e, where):
        score = lax.dot_general(q_s[p, e], k_s[p, e, where], (((1,), (1,)), ((), ())), preferred_element_type=F32)
        return mm(jnp.exp2(score).astype(BF16), v_s[p, where])

    loads[2].wait()
    mine_rows, halo_rows = slice(0, TOKENS), slice(TOKENS, TOKENS + HALO)
    rows = normed(tok[...])
    kr, kc = own_places((TOKENS, 128))
    f = iota((TOKENS, 128), 1)

    def query_marks(base):
        g = f - base
        hit = ((g >= 0) & (g < 16) & (g == kr)) | ((g >= 16) & (g < 32) & (g - 16 == kc))
        return jnp.where(hit, 1.0, 0.0)

    even, odd = query_marks(64), query_marks(0)
    for p in range(3):
        scales = jnp.where(left, scale_ref[2 * p], scale_ref[2 * p + 1]) * math.log2(math.e)
        query = unit(mm(rows, qkv[:, 128 * p:128 * (p + 1)])) * scales
        q_s[p, 0] = jnp.where(left, query, even).astype(BF16)
        q_s[p, 1] = jnp.where(left, odd, query).astype(BF16)
    put_keys(rows, mine_rows, kr, kc, kr >= 0)
    for p in range(3):
        for e in range(2):
            acc[p, e] = attend(p, e, mine_rows)

    for i, (dr, dc, _, _, _) in enumerate(SENDS):
        @pl.when(there(-dr, -dc))
        def _():
            halo_copy(i).wait_recv()

    put_keys(normed(halo[...]), halo_rows, *halo_places((HALO, 128), grid_row, grid_col))

    loads[3].wait()
    for i in range(3):
        p = jnp.where(core == 0, 2 - i, i)
        r0 = acc[p, 0] + attend(p, 0, halo_rows)
        r1_ = acc[p, 1] + attend(p, 1, halo_rows)
        pair = jnp.where(left, r0[:, :128] / r0[:, 128:], r1_[:, :128] / r1_[:, 128:]).astype(BF16)
        att[p] = pair
        grad = lax.dot_general(pair, cot[...], (((0,), (0,)), ((), ())), preferred_element_type=F32)
        if i == 0:
            into = pl.multiple_of(jnp.where(core == 0, 64, 0), 64)
            sent[0:128] = grad.astype(BF16)
            pltpu.make_async_remote_copy(
                src_ref=sent.at[pl.ds(0, 128)], dst_ref=cross.at[pl.ds(into, 128)],
                send_sem=cross_s, recv_sem=cross_r, device_id=partner, device_id_type=MESH,
            ).start()
        elif i == 1:
            upper, lower = grad[0:64], grad[64:128]
            sent[128:192] = jnp.where(core == 0, lower, upper).astype(BF16)
            into = pl.multiple_of(jnp.where(core == 0, 0, 128), 64)
            pltpu.make_async_remote_copy(
                src_ref=sent.at[pl.ds(128, 64)], dst_ref=cross.at[pl.ds(into, 64)],
                send_sem=cross_s, recv_sem=cross_r, device_id=partner, device_id_type=MESH,
            ).start()
            keep = pl.multiple_of(jnp.where(core == 0, 128, 0), 64)
            own[pl.ds(keep, 64)] = jnp.where(core == 0, upper, lower)
        else:
            keep = pl.multiple_of(jnp.where(core == 0, 0, 64), 64)
            own[pl.ds(keep, 128)] = grad
    pltpu.make_async_copy(cross, cross, cross_r).wait()
    pltpu.make_async_copy(cross, cross, cross_s).wait()
    sent[...] = (own[...] + cross[...].astype(F32)).astype(BF16)

    def to_owner(i, _):
        k = lax.rem(mine + i, OWNERS)
        ox, oy = owner_of(k, core)

        @pl.when(k != mine)
        def _():
            pltpu.make_async_remote_copy(
                src_ref=sent.at[pl.ds(pl.multiple_of(k * ROWS, ROWS), ROWS)], dst_ref=part.at[chip],
                send_sem=s1, recv_sem=r1, device_id=device(ox, oy, core, z), device_id_type=MESH,
            ).start()
        return 0

    lax.fori_loop(0, OWNERS, to_owner, 0)

    loads[4].wait()
    branch = mm(att[0], out_w[0:128]) + mm(att[1], out_w[128:256]) + mm(att[2], out_w[256:384])
    upd_ref[...] = (tok[...].astype(F32) + branch).astype(BF16)

    def total_of(ref, count):
        total = ref[0].astype(F32)
        for i in range(1, count):
            total = total + ref[i].astype(F32)
        return total.astype(BF16)

    @pl.when(owns)
    def _():
        part[chip] = sent[pl.ds(pl.multiple_of(mine * ROWS, ROWS), ROWS)]
        pltpu.make_async_copy(part.at[pl.ds(0, 15)], part.at[pl.ds(0, 15)], r1).wait()
        z1[b] = total_of(part, 16)
        for i in range(1, 4):
            pltpu.make_async_remote_copy(
                src_ref=z1.at[b], dst_ref=z1.at[b], send_sem=sz1, recv_sem=rz1,
                device_id=device(x, y, core, a * 4 + lax.rem(b + i, 4)), device_id_type=MESH,
            ).start()
        pltpu.make_async_copy(z1.at[pl.ds(0, 3)], z1.at[pl.ds(0, 3)], rz1).wait()
        z2[a] = total_of(z1, 4)
        for i in range(1, 4):
            pltpu.make_async_remote_copy(
                src_ref=z2.at[a], dst_ref=z2.at[a], send_sem=sz2, recv_sem=rz2,
                device_id=device(x, y, core, lax.rem(a + i, 4) * 4 + b), device_id_type=MESH,
            ).start()
        pltpu.make_async_copy(z2.at[pl.ds(0, 3)], z2.at[pl.ds(0, 3)], rz2).wait()
        row = pl.multiple_of(core * HALF + mine * ROWS, ROWS)
        gath[pl.ds(row, ROWS)] = total_of(z2, 4)

        def spread(i, _):
            c = lax.rem(chip + i, 16)
            pltpu.make_async_remote_copy(
                src_ref=gath.at[pl.ds(row, ROWS)], dst_ref=gath.at[pl.ds(row, ROWS)],
                send_sem=s3, recv_sem=r3.at[mine], device_id=device(c // 4, lax.rem(c, 4), core, z), device_id_type=MESH,
            ).start()
            return 0

        lax.fori_loop(1, 16, spread, 0)

    def forward(i, _):
        k = lax.rem(mine + i, OWNERS)
        block = gath.at[pl.ds(pl.multiple_of(core * HALF + k * ROWS, ROWS), ROWS)]

        @pl.when(k != mine)
        def _():
            pltpu.make_async_copy(block, block, r3.at[k]).wait()

        pltpu.make_async_remote_copy(
            src_ref=block, dst_ref=block, send_sem=s4, recv_sem=r4, device_id=partner, device_id_type=MESH,
        ).start()
        return 0

    lax.fori_loop(0, OWNERS, forward, 0)
    half = gath.at[pl.ds(0, HALF)]
    pltpu.make_async_copy(half, half, r4).wait()
    grad_ref[...] = gath[...].astype(F32)

    pltpu.make_async_copy(half, half, s4).wait()
    for i, (dr, dc, _, _, _) in enumerate(SENDS):
        @pl.when(there(dr, dc))
        def _():
            halo_copy(i).wait_send()

    @pl.when(owns)
    def _():
        pltpu.make_async_copy(sent.at[pl.ds(0, HALF - ROWS)], sent.at[pl.ds(0, HALF - ROWS)], s1).wait()
        pltpu.make_async_copy(z1.at[pl.ds(0, 3)], z1.at[pl.ds(0, 3)], sz1).wait()
        pltpu.make_async_copy(z2.at[pl.ds(0, 3)], z2.at[pl.ds(0, 3)], sz2).wait()
        pltpu.make_async_copy(part.at[pl.ds(0, 15)], part.at[pl.ds(0, 15)], s3).wait()

    @pl.when(jnp.logical_not(owns))
    def _():
        pltpu.make_async_copy(sent, sent, s1).wait()


def body(tokens, timesteps, cond_weight, qkv_weight, head_scale, out_weight, cotangent):
    anywhere = pl.BlockSpec(memory_space=pltpu.HBM)
    whole = pl.BlockSpec(memory_space=pltpu.VMEM)
    dma = pltpu.SemaphoreType.DMA
    updated, grad = pl.pallas_call(
        kernel,
        out_shape=(pltpu.VMEM((TOKENS, CH), BF16), pltpu.VMEM((CH, CH), F32)),
        in_specs=[anywhere] * 6 + [pl.BlockSpec(memory_space=pltpu.SMEM)],
        out_specs=(whole, whole),
        scratch_shapes=[
            pltpu.VMEM((TOKENS, CH), BF16),
            pltpu.VMEM((TOKENS, CH), BF16),
            pltpu.VMEM((CH, 3 * CH), BF16),
            pltpu.VMEM((CH, CH), BF16),
            pltpu.VMEM((256, CH), BF16),
            pltpu.SMEM((6,), F32),
            pltpu.VMEM((160, CH), BF16),
            pltpu.VMEM((HALO, CH), BF16),
            pltpu.VMEM((3, 2, TOKENS, 128), BF16),
            pltpu.VMEM((3, 2, TOKENS + HALO, 128), BF16),
            pltpu.VMEM((3, TOKENS + HALO, 256), BF16),
            pltpu.VMEM((3, 2, TOKENS, 256), F32),
            pltpu.VMEM((3, TOKENS, 128), BF16),
            pltpu.VMEM((HALF, CH), F32),
            pltpu.VMEM((HALF, CH), BF16),
            pltpu.VMEM((HALF, CH), BF16),
            pltpu.VMEM((16, ROWS, CH), BF16),
            pltpu.VMEM((4, ROWS, CH), BF16),
            pltpu.VMEM((4, ROWS, CH), BF16),
            pltpu.VMEM((CH, CH), BF16),
            dma((6,)), dma(()), dma((8,)),
        ] + [dma(())] * 9 + [dma((OWNERS,)), dma(()), dma(())],
        compiler_params=pltpu.CompilerParams(collective_id=0, has_side_effects=True, vmem_limit_bytes=40 * 2**20),
    )(*(
        pltpu.with_memory_space_constraint(array, pltpu.HBM)
        for array in (
            tokens.reshape(TOKENS, CH), cotangent.reshape(TOKENS, CH),
            qkv_weight, out_weight, cond_weight, head_scale,
        )
    ), timesteps)
    return updated.reshape(tokens.shape), grad


def solution(mesh):
    return jax.shard_map(
        body,
        mesh=mesh,
        in_specs=(
            P("dp", "tile", None, None, None),
            P("dp"),
            P(),
            P(),
            P(),
            P(),
            P("dp", "tile", None, None, None),
        ),
        out_specs=(P("dp", "tile", None, None, None), P()),
        check_vma=False,
    )
```

```python
import math

import jax
import jax.numpy as jnp
from jax import lax
from jax.experimental import pallas as pl
from jax.experimental.pallas import tpu as pltpu
from jax.sharding import PartitionSpec as P

MESH = pl.DeviceIdType.MESH
F32, BF16 = jnp.float32, jnp.bfloat16
TOKENS = 256
CH = 384
HALO = 384
PART = 128
STRIP = 48
ROWS = 16
OWNERS = 12
HALF = OWNERS * ROWS
FAR = -16384.0
SENDS = (
    (1, 0, 208, 48, 0),
    (-1, 0, 0, 48, 128),
    (1, 1, 96, 16, 48),
    (1, -1, 112, 16, 64),
    (-1, 1, 128, 16, 176),
    (-1, -1, 144, 16, 192),
    (0, 1, 0, 48, 256),
    (0, -1, 48, 48, 304),
)

STEPS = sorted(
    ((i, j) for i in range(4) for j in range(4) if i or j), key=lambda s: (-min(s[0], 4 - s[0]) - min(s[1], 4 - s[1]), s)
)


def mm(a, b):
    return jnp.dot(a, b, preferred_element_type=F32)


def iota(shape, axis):
    return lax.broadcasted_iota(jnp.int32, shape, axis)


def thirds(m):
    return (m >= 3).astype(jnp.int32) + (m >= 6).astype(jnp.int32) + (m >= 9).astype(jnp.int32)


def pick_matrix():
    r = iota((160, TOKENS), 0)
    m48 = jnp.where(r >= 48, r - 48, r)
    side = (m48 % 16) * 16 + m48 // 16 + jnp.where(r < 48, 13, 0)
    m = r % 16
    third = thirds(m)
    corner = third * 16 + m - 3 * third + jnp.where(r < 128, 13 * 16, 0)
    corner = corner + jnp.where((r < 112) | ((r >= 128) & (r < 144)), 13, 0)
    corner = jnp.where(m < 9, corner, -1)
    wanted = jnp.where(r < 96, side, corner)
    return jnp.where(iota((160, TOKENS), 1) == wanted, 1.0, 0.0).astype(BF16)


def key_marks(kr, kc, known, base):
    f = iota(kr.shape, 1) - base
    apart = jnp.where(f < 16, jnp.abs(kr - f), jnp.abs(kc - (f - 16)))
    bad = (apart > 3) | jnp.logical_not(known)
    return jnp.where(bad & (f >= 0) & (f < 32), FAR, 0.0)


def own_places(shape):
    i = iota(shape, 0)
    return i // 16, i % 16


def side_places(grid_col):
    j = iota((PART, 128), 0)
    west = j < 48
    m = jnp.where(west, j, j - 48)
    known = (j < 96) & ((west & (grid_col > 0)) | (jnp.logical_not(west) & (grid_col < 3)))
    return m % 16, m // 16 + jnp.where(west, -3, 16), known


def strip_places(top, grid_row, grid_col):
    j = iota((PART, 128), 0)
    c = j % 16
    third = thirds(c)
    corner, west = j >= 48, j < 64
    kr = jnp.where(corner, third, j // 16) + jnp.where(top, -3, 16)
    kc = jnp.where(corner, c - 3 * third + jnp.where(west, -3, 16), c)
    known = (west & (grid_col > 0)) | (jnp.logical_not(west) & (grid_col < 3))
    known = jnp.logical_not(corner) | (known & (c < 9) & (j < 80))
    beyond = jnp.where(top, grid_row > 0, grid_row < 3)
    return kr, kc, known & beyond


def device(x, y, core, z):
    return (x * 8 + lax.rem(z, 8), (z // 8) * 8 + y * 2 + core)


def owned_by(x, y, core):
    y = jnp.where(core == 0, y, 3 - y)
    return jnp.where(x == y, OWNERS, x * 3 + y - jnp.where(y > x, 1, 0))


def kernel(
    tok_hbm, cot_hbm, qkv_hbm, out_w_hbm, cond_hbm, scale_hbm, step_ref,
    upd_ref, grad_ref,
    tok, cot, qkv, out_w, cond, scale_ref, packed, halo, q_s, k_s, v_s, acc, att, early,
    own, cross, sent, part, z1, z2, gath,
    in_sem, halo_s, halo_r, cross_s, cross_r, s1, r1, sz1, rz1, sz2, rz2, s3, r3, s4, r4,
):
    dp, tile = lax.axis_index("dp"), lax.axis_index("tile")
    grid_row, grid_col = tile // 4, lax.rem(tile, 4)
    x, z = dp // 8, (tile // 8) * 8 + lax.rem(dp, 8)
    y, core = lax.rem(tile, 8) // 2, lax.rem(tile, 2)
    a, b = z // 4, lax.rem(z, 4)
    chip = x * 4 + y
    mine = owned_by(x, y, core)
    owns = mine < OWNERS
    partner = (dp, tile + 1 - 2 * core)

    loads = [
        pltpu.make_async_copy(src, dst, in_sem.at[i])
        for i, (src, dst) in enumerate(((tok_hbm, tok), (cond_hbm, cond), (qkv_hbm, qkv), (cot_hbm, cot), (out_w_hbm, out_w), (scale_hbm, scale_ref)))
    ]
    halo[...] = jnp.zeros_like(halo)
    barrier = pltpu.get_barrier_semaphore()

    def there(dr, dc):
        ok = True
        if dr:
            ok = (grid_row < 3) if dr > 0 else (grid_row > 0)
        if dc:
            right = (grid_col < 3) if dc > 0 else (grid_col > 0)
            ok = (ok & right) if dr else right
        return ok

    near = 0
    for dr, dc, _, _, _ in SENDS:
        ok = there(dr, dc)
        near = near + jnp.where(ok, 1, 0)

        @pl.when(ok)
        def _():
            pl.semaphore_signal(barrier, inc=1, device_id=(dp, tile + 4 * dr + dc), device_id_type=MESH)

    for load in loads:
        load.start()
    pl.semaphore_signal(barrier, inc=1, device_id=partner, device_id_type=MESH)
    for i in range(1, 4):
        pl.semaphore_signal(barrier, inc=1, device_id=device(x, y, core, a * 4 + lax.rem(b + i, 4)), device_id_type=MESH)
        pl.semaphore_signal(barrier, inc=1, device_id=device(x, y, core, lax.rem(a + i, 4) * 4 + b), device_id_type=MESH)

    for i, j in STEPS:
        pl.semaphore_signal(barrier, inc=1, device_id=device(lax.rem(x + i, 4), lax.rem(y + j, 4), core, z), device_id_type=MESH)

    loads[0].wait()
    packed[...] = mm(pick_matrix(), tok[...]).astype(BF16)

    pl.semaphore_wait(barrier, 22 + near)

    def halo_copy(i):
        dr, dc, place, count, into = SENDS[i]
        source = tok if dc == 0 else packed
        return pltpu.make_async_remote_copy(
            src_ref=source.at[pl.ds(place, count)], dst_ref=halo.at[pl.ds(into, count)],
            send_sem=halo_s, recv_sem=halo_r.at[i], device_id=(dp, tile + 4 * dr + dc), device_id_type=MESH,
        )

    for i, (dr, dc, _, _, _) in enumerate(SENDS):
        @pl.when(there(dr, dc))
        def _():
            halo_copy(i).start()

    loads[1].wait()
    loads[5].wait()
    frequency = jnp.exp((-math.log(10000.0) / 128) * iota((8, 128), 1).astype(F32))
    angles = step_ref[0].astype(F32) * frequency
    features = jnp.concatenate([jnp.cos(angles), jnp.sin(angles)], axis=1)
    high = features.astype(BF16)
    rest = features - high.astype(F32)
    middle = rest.astype(BF16)
    low = (rest - middle.astype(F32)).astype(BF16)
    gain = 1.0 + mm(high, cond[...]) + mm(middle, cond[...]) + mm(low, cond[...])
    gain = gain[0:1]

    same_head = jnp.where((iota((128, 128), 0) < 64) == (iota((128, 128), 1) < 64), 1.0, 0.0).astype(BF16)
    same_head = jnp.concatenate([same_head, same_head], axis=0)

    def normed(rows):
        wide = rows.astype(F32)
        mean_square = jnp.mean(wide * wide, axis=-1, keepdims=True)
        return (wide * lax.rsqrt(mean_square + 1e-06) * gain).astype(BF16)

    def unit(vectors):
        square = vectors * vectors
        high = square.astype(BF16)
        low = (square - high.astype(F32)).astype(BF16)
        total = mm(jnp.concatenate([high, low], axis=1), same_head)
        return vectors * lax.rsqrt(total + 1e-06)

    def left_of(count):
        return iota((count, 128), 1) < 64

    def put_keys(rows, begin, places):
        count = rows.shape[0]
        where, left = slice(begin, begin + count), left_of(count)
        even, odd = key_marks(*places, 64), key_marks(*places, 0)
        for p in range(3):
            key = unit(mm(rows, qkv[:, CH + 128 * p:CH + 128 * (p + 1)]))
            k_s[p, 0, where] = jnp.where(left, key, even).astype(BF16)
            k_s[p, 1, where] = jnp.where(left, odd, key).astype(BF16)
            value = mm(rows, qkv[:, 2 * CH + 128 * p:2 * CH + 128 * (p + 1)])
            v_s[p, where, 0:128] = value.astype(BF16)
            v_s[p, where, 128:256] = jnp.ones((count, 128), BF16)

    def attend(p, e, queries, begin, count):
        keys = slice(begin, begin + count)
        score = lax.dot_general(q_s[p, e, queries], k_s[p, e, keys], (((1,), (1,)), ((), ())), preferred_element_type=F32)
        return mm(jnp.exp2(score).astype(BF16), v_s[p, keys])

    def shares(r0, r1):
        left = left_of(r0.shape[0])
        return jnp.where(left, r0[:, :128] / r0[:, 128:], r1[:, :128] / r1[:, 128:]).astype(BF16)

    def outer(rows, cots):
        return lax.dot_general(rows, cots, (((0,), (0,)), ((), ())), preferred_element_type=F32)

    def await_halo(steps, wanted):
        for i, (dr, dc, _, _, _) in enumerate(SENDS):
            if dr not in steps:
                continue

            @pl.when(there(-dr, -dc) & wanted(dr))
            def _():
                halo_copy(i).wait_recv()

    loads[2].wait()
    rows = normed(tok[...])
    kr, kc = own_places((TOKENS, 128))
    f = iota((TOKENS, 128), 1)

    def query_marks(base):
        g = f - base
        hit = ((g >= 0) & (g < 16) & (g == kr)) | ((g >= 16) & (g < 32) & (g - 16 == kc))
        return jnp.where(hit, 1.0, 0.0)

    even, odd = query_marks(64), query_marks(0)
    left = left_of(TOKENS)
    for p in range(3):
        scales = jnp.where(left, scale_ref[2 * p], scale_ref[2 * p + 1]) * math.log2(math.e)
        query = unit(mm(rows, qkv[:, 128 * p:128 * (p + 1)])) * scales
        q_s[p, 0] = jnp.where(left, query, even).astype(BF16)
        q_s[p, 1] = jnp.where(left, odd, query).astype(BF16)
    put_keys(rows, 0, (kr, kc, kr >= 0))
    every = slice(0, TOKENS)
    for p in range(3):
        for e in range(2):
            acc[p, e] = attend(p, e, every, 0, TOKENS)

    await_halo((0,), lambda dr: True)
    put_keys(normed(halo[2 * PART:3 * PART]), TOKENS, side_places(grid_col))
    for p in range(3):
        for e in range(2):
            acc[p, e] += attend(p, e, every, TOKENS, PART)

    top_last = lax.rem(grid_row, 2) == 0
    await_halo((-1, 1), lambda dr: top_last if dr < 0 else jnp.logical_not(top_last))
    near_rows = pl.multiple_of(jnp.where(top_last, PART, 0), PART)
    put_keys(normed(halo[pl.ds(near_rows, PART)]), TOKENS + PART, strip_places(jnp.logical_not(top_last), grid_row, grid_col))
    near_queries = pl.ds(pl.multiple_of(jnp.where(top_last, TOKENS - STRIP, 0), 16), STRIP)
    for p in range(3):
        for e in range(2):
            acc[p, e, near_queries] += attend(p, e, near_queries, TOKENS + PART, PART)

    loads[3].wait()
    done = pl.ds(pl.multiple_of(jnp.where(top_last, STRIP, 0), 16), TOKENS - STRIP)
    for p in range(3):
        att[p] = shares(acc[p, 0], acc[p, 1])
        early[p] = outer(att[p, done], cot[done])

    far_rows = pl.multiple_of(jnp.where(top_last, 0, PART), PART)
    far_queries = pl.ds(pl.multiple_of(jnp.where(top_last, 0, TOKENS - STRIP), 16), STRIP)
    places = strip_places(top_last, grid_row, grid_col)
    await_halo((-1, 1), lambda dr: jnp.logical_not(top_last) if dr < 0 else top_last)
    put_keys(normed(halo[pl.ds(far_rows, PART)]), TOKENS + 2 * PART, places)
    late = [
        [acc[p, e, far_queries] + attend(p, e, far_queries, TOKENS + 2 * PART, PART) for e in range(2)] for p in range(3)
    ]
    pairs = [shares(*r) for r in late]
    far_cot = cot[far_queries]
    grads = [early[p] + outer(pairs[p], far_cot) for p in range(3)]
    first = jnp.concatenate([grads[0], grads[1][0:64]], axis=0)
    second = jnp.concatenate([grads[1][64:128], grads[2]], axis=0)
    sent[...] = jnp.where(core == 0, second, first).astype(BF16)
    over = pltpu.make_async_remote_copy(
        src_ref=sent, dst_ref=cross, send_sem=cross_s, recv_sem=cross_r, device_id=partner, device_id_type=MESH,
    )
    over.start()
    own[...] = jnp.where(core == 0, first, second)
    for p in range(3):
        att[p, far_queries] = pairs[p]
    over.wait()
    sent[...] = (own[...] + cross[...].astype(F32)).astype(BF16)

    for i, j in STEPS:
        ox, oy = lax.rem(x + i, 4), lax.rem(y + j, 4)
        k = owned_by(ox, oy, core)

        @pl.when(k < OWNERS)
        def _():
            pltpu.make_async_remote_copy(
                src_ref=sent.at[pl.ds(pl.multiple_of(k * ROWS, ROWS), ROWS)], dst_ref=part.at[chip],
                send_sem=s1, recv_sem=r1, device_id=device(ox, oy, core, z), device_id_type=MESH,
            ).start()

    loads[4].wait()
    branch = mm(att[0], out_w[0:128]) + mm(att[1], out_w[128:256]) + mm(att[2], out_w[256:384])
    upd_ref[...] = (tok[...].astype(F32) + branch).astype(BF16)

    def total_of(ref, count):
        total = ref[0].astype(F32)
        for i in range(1, count):
            total = total + ref[i].astype(F32)
        return total.astype(BF16)

    @pl.when(owns)
    def _():
        part[chip] = sent[pl.ds(pl.multiple_of(mine * ROWS, ROWS), ROWS)]
        pltpu.make_async_copy(part.at[pl.ds(0, 15)], part.at[pl.ds(0, 15)], r1).wait()
        z1[b] = total_of(part, 16)
        for i in range(1, 4):
            pltpu.make_async_remote_copy(
                src_ref=z1.at[b], dst_ref=z1.at[b], send_sem=sz1, recv_sem=rz1,
                device_id=device(x, y, core, a * 4 + lax.rem(b + i, 4)), device_id_type=MESH,
            ).start()
        pltpu.make_async_copy(z1.at[pl.ds(0, 3)], z1.at[pl.ds(0, 3)], rz1).wait()
        z2[a] = total_of(z1, 4)
        for i in range(1, 4):
            pltpu.make_async_remote_copy(
                src_ref=z2.at[a], dst_ref=z2.at[a], send_sem=sz2, recv_sem=rz2,
                device_id=device(x, y, core, lax.rem(a + i, 4) * 4 + b), device_id_type=MESH,
            ).start()
        pltpu.make_async_copy(z2.at[pl.ds(0, 3)], z2.at[pl.ds(0, 3)], rz2).wait()
        row = pl.multiple_of(core * HALF + mine * ROWS, ROWS)
        gath[pl.ds(row, ROWS)] = total_of(z2, 4)

        for i, j in STEPS:
            pltpu.make_async_remote_copy(
                src_ref=gath.at[pl.ds(row, ROWS)], dst_ref=gath.at[pl.ds(row, ROWS)], send_sem=s3,
                recv_sem=r3.at[mine], device_id=device(lax.rem(x + i, 4), lax.rem(y + j, 4), core, z), device_id_type=MESH,
            ).start()

    for i, j in ((0, 0),) + tuple(reversed(STEPS)):
        k = owned_by(lax.rem(x + i, 4), lax.rem(y + j, 4), core)

        @pl.when(k < OWNERS)
        def _():
            block = gath.at[pl.ds(pl.multiple_of(core * HALF + k * ROWS, ROWS), ROWS)]
            if i or j:
                pltpu.make_async_copy(block, block, r3.at[k]).wait()
            pltpu.make_async_remote_copy(
                src_ref=block, dst_ref=block, send_sem=s4, recv_sem=r4, device_id=partner, device_id_type=MESH,
            ).start()

    half = gath.at[pl.ds(0, HALF)]
    pltpu.make_async_copy(half, half, r4).wait()
    grad_ref[...] = gath[...].astype(F32)

    pltpu.make_async_copy(half, half, s4).wait()
    for i, (dr, dc, _, _, _) in enumerate(SENDS):
        @pl.when(there(dr, dc))
        def _():
            halo_copy(i).wait_send()

    @pl.when(owns)
    def _():
        pltpu.make_async_copy(sent.at[pl.ds(0, HALF - ROWS)], sent.at[pl.ds(0, HALF - ROWS)], s1).wait()
        pltpu.make_async_copy(z1.at[pl.ds(0, 3)], z1.at[pl.ds(0, 3)], sz1).wait()
        pltpu.make_async_copy(z2.at[pl.ds(0, 3)], z2.at[pl.ds(0, 3)], sz2).wait()
        pltpu.make_async_copy(part.at[pl.ds(0, 15)], part.at[pl.ds(0, 15)], s3).wait()

    @pl.when(jnp.logical_not(owns))
    def _():
        pltpu.make_async_copy(sent, sent, s1).wait()


def hand_over(upd_ref, grad_ref, upd_hbm, grad_hbm, sems):
    copies = [
        pltpu.make_async_copy(grad_ref, grad_hbm, sems.at[0]),
        pltpu.make_async_copy(upd_ref, upd_hbm, sems.at[1]),
    ]
    for copy in copies:
        copy.start()
    for copy in copies:
        copy.wait()


def body(tokens, timesteps, cond_weight, qkv_weight, head_scale, out_weight, cotangent):
    anywhere = pl.BlockSpec(memory_space=pltpu.HBM)
    whole = pl.BlockSpec(memory_space=pltpu.VMEM)
    dma = pltpu.SemaphoreType.DMA
    updated, grad = pl.pallas_call(
        kernel,
        out_shape=(pltpu.VMEM((TOKENS, CH), BF16), pltpu.VMEM((CH, CH), F32)),
        in_specs=[anywhere] * 6 + [pl.BlockSpec(memory_space=pltpu.SMEM)],
        out_specs=(whole, whole),
        scratch_shapes=[
            pltpu.VMEM((TOKENS, CH), BF16),
            pltpu.VMEM((TOKENS, CH), BF16),
            pltpu.VMEM((CH, 3 * CH), BF16),
            pltpu.VMEM((CH, CH), BF16),
            pltpu.VMEM((256, CH), BF16),
            pltpu.SMEM((6,), F32),
            pltpu.VMEM((160, CH), BF16),
            pltpu.VMEM((HALO, CH), BF16),
            pltpu.VMEM((3, 2, TOKENS, 128), BF16),
            pltpu.VMEM((3, 2, TOKENS + HALO, 128), BF16),
            pltpu.VMEM((3, TOKENS + HALO, 256), BF16),
            pltpu.VMEM((3, 2, TOKENS, 256), F32),
            pltpu.VMEM((3, TOKENS, 128), BF16),
            pltpu.VMEM((3, 128, CH), F32),
            pltpu.VMEM((HALF, CH), F32),
            pltpu.VMEM((HALF, CH), BF16),
            pltpu.VMEM((HALF, CH), BF16),
            pltpu.VMEM((16, ROWS, CH), BF16),
            pltpu.VMEM((4, ROWS, CH), BF16),
            pltpu.VMEM((4, ROWS, CH), BF16),
            pltpu.VMEM((CH, CH), BF16),
            dma((6,)), dma(()), dma((8,)),
        ] + [dma(())] * 9 + [dma((OWNERS,)), dma(()), dma(())],
        compiler_params=pltpu.CompilerParams(collective_id=0, has_side_effects=True, vmem_limit_bytes=40 * 2**20),
    )(*(
        pltpu.with_memory_space_constraint(array, pltpu.HBM)
        for array in (
            tokens.reshape(TOKENS, CH), cotangent.reshape(TOKENS, CH),
            qkv_weight, out_weight, cond_weight, head_scale,
        )
    ), timesteps)
    updated, grad = pl.pallas_call(
        hand_over,
        out_shape=(pltpu.HBM((TOKENS, CH), BF16), pltpu.HBM((CH, CH), F32)),
        in_specs=[pl.BlockSpec(memory_space=pl.ANY)] * 2,
        out_specs=(pl.BlockSpec(memory_space=pl.ANY),) * 2,
        scratch_shapes=[dma((2,))],
    )(pltpu.with_memory_space_constraint(updated, pltpu.VMEM), pltpu.with_memory_space_constraint(grad, pltpu.VMEM))
    return updated.reshape(tokens.shape), grad


def solution(mesh):
    return jax.shard_map(
        body,
        mesh=mesh,
        in_specs=(
            P("dp", "tile", None, None, None),
            P("dp"),
            P(),
            P(),
            P(),
            P(),
            P("dp", "tile", None, None, None),
        ),
        out_specs=(P("dp", "tile", None, None, None), P()),
        check_vma=False,
    )
```

```python
import math

import jax
import jax.numpy as jnp
from jax import lax
from jax.experimental import pallas as pl
from jax.experimental.pallas import tpu as pltpu
from jax.sharding import PartitionSpec as P

MESH = pl.DeviceIdType.MESH
F32, BF16 = jnp.float32, jnp.bfloat16
TOKENS = 256
CH = 384
HALO = 384
PART = 128
STRIP = 48
ROWS = 16
OWNERS = 12
HALF = OWNERS * ROWS
FAR = -16384.0
SENDS = (
    (1, 0, 208, 48, 0),
    (-1, 0, 0, 48, 128),
    (1, 1, 96, 16, 48),
    (1, -1, 112, 16, 64),
    (-1, 1, 128, 16, 176),
    (-1, -1, 144, 16, 192),
    (0, 1, 0, 48, 256),
    (0, -1, 48, 48, 304),
)

STEPS = sorted(
    ((i, j) for i in range(4) for j in range(4) if i or j), key=lambda s: (-min(s[0], 4 - s[0]) - min(s[1], 4 - s[1]), s)
)

ALONG = sorted(range(1, 16), key=lambda i: -min(i, 16 - i))


def mm(a, b):
    return jnp.dot(a, b, preferred_element_type=F32)


def iota(shape, axis):
    return lax.broadcasted_iota(jnp.int32, shape, axis)


def thirds(m):
    return (m >= 3).astype(jnp.int32) + (m >= 6).astype(jnp.int32) + (m >= 9).astype(jnp.int32)


def pick_matrix():
    r = iota((160, TOKENS), 0)
    m48 = jnp.where(r >= 48, r - 48, r)
    side = (m48 % 16) * 16 + m48 // 16 + jnp.where(r < 48, 13, 0)
    m = r % 16
    third = thirds(m)
    corner = third * 16 + m - 3 * third + jnp.where(r < 128, 13 * 16, 0)
    corner = corner + jnp.where((r < 112) | ((r >= 128) & (r < 144)), 13, 0)
    corner = jnp.where(m < 9, corner, -1)
    wanted = jnp.where(r < 96, side, corner)
    return jnp.where(iota((160, TOKENS), 1) == wanted, 1.0, 0.0).astype(BF16)


def key_marks(kr, kc, known, base):
    f = iota(kr.shape, 1) - base
    apart = jnp.where(f < 16, jnp.abs(kr - f), jnp.abs(kc - (f - 16)))
    bad = (apart > 3) | jnp.logical_not(known)
    return jnp.where(bad & (f >= 0) & (f < 32), FAR, 0.0)


def own_places(shape):
    i = iota(shape, 0)
    return i // 16, i % 16


def side_places(grid_col):
    j = iota((PART, 128), 0)
    west = j < 48
    m = jnp.where(west, j, j - 48)
    known = (j < 96) & ((west & (grid_col > 0)) | (jnp.logical_not(west) & (grid_col < 3)))
    return m % 16, m // 16 + jnp.where(west, -3, 16), known


def strip_places(top, grid_row, grid_col):
    j = iota((PART, 128), 0)
    c = j % 16
    third = thirds(c)
    corner, west = j >= 48, j < 64
    kr = jnp.where(corner, third, j // 16) + jnp.where(top, -3, 16)
    kc = jnp.where(corner, c - 3 * third + jnp.where(west, -3, 16), c)
    known = (west & (grid_col > 0)) | (jnp.logical_not(west) & (grid_col < 3))
    known = jnp.logical_not(corner) | (known & (c < 9) & (j < 80))
    beyond = jnp.where(top, grid_row > 0, grid_row < 3)
    return kr, kc, known & beyond


def device(x, y, core, z):
    return (x * 8 + lax.rem(z, 8), (z // 8) * 8 + y * 2 + core)


def owned_by(x, y, core):
    y = jnp.where(core == 0, y, 3 - y)
    return jnp.where(x == y, OWNERS, x * 3 + y - jnp.where(y > x, 1, 0))


def kernel(
    tok_hbm, cot_hbm, qkv_hbm, out_w_hbm, cond_hbm, scale_hbm, step_ref,
    upd_ref, grad_ref,
    tok, cot, qkv, out_w, cond, scale_ref, packed, halo, q_s, k_s, v_s, acc, att, early,
    own, cross, sent, part, z1, gath,
    in_sem, halo_s, halo_r, cross_s, cross_r, s1, r1, sz1, rz1, s3, r3, s4, r4,
):
    dp, tile = lax.axis_index("dp"), lax.axis_index("tile")
    grid_row, grid_col = tile // 4, lax.rem(tile, 4)
    x, z = dp // 8, (tile // 8) * 8 + lax.rem(dp, 8)
    y, core = lax.rem(tile, 8) // 2, lax.rem(tile, 2)
    chip = x * 4 + y
    mine = owned_by(x, y, core)
    owns = mine < OWNERS
    partner = (dp, tile + 1 - 2 * core)

    loads = [
        pltpu.make_async_copy(src, dst, in_sem.at[i])
        for i, (src, dst) in enumerate(((tok_hbm, tok), (cond_hbm, cond), (qkv_hbm, qkv), (cot_hbm, cot), (out_w_hbm, out_w), (scale_hbm, scale_ref)))
    ]
    halo[...] = jnp.zeros_like(halo)
    barrier = pltpu.get_barrier_semaphore()

    def there(dr, dc):
        ok = True
        if dr:
            ok = (grid_row < 3) if dr > 0 else (grid_row > 0)
        if dc:
            right = (grid_col < 3) if dc > 0 else (grid_col > 0)
            ok = (ok & right) if dr else right
        return ok

    near = 0
    for dr, dc, _, _, _ in SENDS:
        ok = there(dr, dc)
        near = near + jnp.where(ok, 1, 0)

        @pl.when(ok)
        def _():
            pl.semaphore_signal(barrier, inc=1, device_id=(dp, tile + 4 * dr + dc), device_id_type=MESH)

    for load in loads:
        load.start()
    pl.semaphore_signal(barrier, inc=1, device_id=partner, device_id_type=MESH)
    for i in ALONG:
        pl.semaphore_signal(barrier, inc=1, device_id=device(x, y, core, lax.rem(z + i, 16)), device_id_type=MESH)
    for i, j in STEPS:
        pl.semaphore_signal(barrier, inc=1, device_id=device(lax.rem(x + i, 4), lax.rem(y + j, 4), core, z), device_id_type=MESH)

    loads[0].wait()
    packed[...] = mm(pick_matrix(), tok[...]).astype(BF16)

    pl.semaphore_wait(barrier, 31 + near)

    def halo_copy(i):
        dr, dc, place, count, into = SENDS[i]
        source = tok if dc == 0 else packed
        return pltpu.make_async_remote_copy(
            src_ref=source.at[pl.ds(place, count)], dst_ref=halo.at[pl.ds(into, count)],
            send_sem=halo_s, recv_sem=halo_r.at[i], device_id=(dp, tile + 4 * dr + dc), device_id_type=MESH,
        )

    for i, (dr, dc, _, _, _) in enumerate(SENDS):
        @pl.when(there(dr, dc))
        def _():
            halo_copy(i).start()

    loads[1].wait()
    loads[5].wait()
    frequency = jnp.exp((-math.log(10000.0) / 128) * iota((8, 128), 1).astype(F32))
    angles = step_ref[0].astype(F32) * frequency
    features = jnp.concatenate([jnp.cos(angles), jnp.sin(angles)], axis=1)
    high = features.astype(BF16)
    rest = features - high.astype(F32)
    middle = rest.astype(BF16)
    low = (rest - middle.astype(F32)).astype(BF16)
    gain = 1.0 + mm(high, cond[...]) + mm(middle, cond[...]) + mm(low, cond[...])
    gain = gain[0:1]

    same_head = jnp.where((iota((128, 128), 0) < 64) == (iota((128, 128), 1) < 64), 1.0, 0.0).astype(BF16)
    same_head = jnp.concatenate([same_head, same_head], axis=0)

    def normed(rows):
        wide = rows.astype(F32)
        mean_square = jnp.mean(wide * wide, axis=-1, keepdims=True)
        return (wide * lax.rsqrt(mean_square + 1e-06) * gain).astype(BF16)

    def unit(vectors):
        square = vectors * vectors
        high = square.astype(BF16)
        low = (square - high.astype(F32)).astype(BF16)
        total = mm(jnp.concatenate([high, low], axis=1), same_head)
        return vectors * lax.rsqrt(total + 1e-06)

    def left_of(count):
        return iota((count, 128), 1) < 64

    def put_keys(rows, begin, places):
        count = rows.shape[0]
        where, left = slice(begin, begin + count), left_of(count)
        even, odd = key_marks(*places, 64), key_marks(*places, 0)
        for p in range(3):
            key = unit(mm(rows, qkv[:, CH + 128 * p:CH + 128 * (p + 1)]))
            k_s[p, 0, where] = jnp.where(left, key, even).astype(BF16)
            k_s[p, 1, where] = jnp.where(left, odd, key).astype(BF16)
            value = mm(rows, qkv[:, 2 * CH + 128 * p:2 * CH + 128 * (p + 1)])
            v_s[p, where, 0:128] = value.astype(BF16)
            v_s[p, where, 128:256] = jnp.ones((count, 128), BF16)

    def attend(p, e, queries, begin, count):
        keys = slice(begin, begin + count)
        score = lax.dot_general(q_s[p, e, queries], k_s[p, e, keys], (((1,), (1,)), ((), ())), preferred_element_type=F32)
        return mm(jnp.exp2(score).astype(BF16), v_s[p, keys])

    def shares(r0, r1):
        left = left_of(r0.shape[0])
        return jnp.where(left, r0[:, :128] / r0[:, 128:], r1[:, :128] / r1[:, 128:]).astype(BF16)

    def outer(rows, cots):
        return lax.dot_general(rows, cots, (((0,), (0,)), ((), ())), preferred_element_type=F32)

    def await_halo(steps, wanted):
        for i, (dr, dc, _, _, _) in enumerate(SENDS):
            if dr not in steps:
                continue

            @pl.when(there(-dr, -dc) & wanted(dr))
            def _():
                halo_copy(i).wait_recv()

    loads[2].wait()
    rows = normed(tok[...])
    kr, kc = own_places((TOKENS, 128))
    f = iota((TOKENS, 128), 1)

    def query_marks(base):
        g = f - base
        hit = ((g >= 0) & (g < 16) & (g == kr)) | ((g >= 16) & (g < 32) & (g - 16 == kc))
        return jnp.where(hit, 1.0, 0.0)

    even, odd = query_marks(64), query_marks(0)
    left = left_of(TOKENS)
    for p in range(3):
        scales = jnp.where(left, scale_ref[2 * p], scale_ref[2 * p + 1]) * math.log2(math.e)
        query = unit(mm(rows, qkv[:, 128 * p:128 * (p + 1)])) * scales
        q_s[p, 0] = jnp.where(left, query, even).astype(BF16)
        q_s[p, 1] = jnp.where(left, odd, query).astype(BF16)
    put_keys(rows, 0, (kr, kc, kr >= 0))
    every = slice(0, TOKENS)
    for p in range(3):
        for e in range(2):
            acc[p, e] = attend(p, e, every, 0, TOKENS)

    await_halo((0,), lambda dr: True)
    put_keys(normed(halo[2 * PART:3 * PART]), TOKENS, side_places(grid_col))
    for p in range(3):
        for e in range(2):
            acc[p, e] += attend(p, e, every, TOKENS, PART)

    top_last = lax.rem(grid_row, 2) == 0
    await_halo((-1, 1), lambda dr: top_last if dr < 0 else jnp.logical_not(top_last))
    near_rows = pl.multiple_of(jnp.where(top_last, PART, 0), PART)
    put_keys(normed(halo[pl.ds(near_rows, PART)]), TOKENS + PART, strip_places(jnp.logical_not(top_last), grid_row, grid_col))
    near_queries = pl.ds(pl.multiple_of(jnp.where(top_last, TOKENS - STRIP, 0), 16), STRIP)
    for p in range(3):
        for e in range(2):
            acc[p, e, near_queries] += attend(p, e, near_queries, TOKENS + PART, PART)

    loads[3].wait()
    done = pl.ds(pl.multiple_of(jnp.where(top_last, STRIP, 0), 16), TOKENS - STRIP)
    for p in range(3):
        att[p] = shares(acc[p, 0], acc[p, 1])
        early[p] = outer(att[p, done], cot[done])

    far_rows = pl.multiple_of(jnp.where(top_last, 0, PART), PART)
    far_queries = pl.ds(pl.multiple_of(jnp.where(top_last, 0, TOKENS - STRIP), 16), STRIP)
    places = strip_places(top_last, grid_row, grid_col)
    await_halo((-1, 1), lambda dr: jnp.logical_not(top_last) if dr < 0 else top_last)
    put_keys(normed(halo[pl.ds(far_rows, PART)]), TOKENS + 2 * PART, places)
    late = [
        [acc[p, e, far_queries] + attend(p, e, far_queries, TOKENS + 2 * PART, PART) for e in range(2)] for p in range(3)
    ]
    pairs = [shares(*r) for r in late]
    far_cot = cot[far_queries]
    grads = [early[p] + outer(pairs[p], far_cot) for p in range(3)]
    first = jnp.concatenate([grads[0], grads[1][0:64]], axis=0)
    second = jnp.concatenate([grads[1][64:128], grads[2]], axis=0)
    sent[...] = jnp.where(core == 0, second, first).astype(BF16)
    over = pltpu.make_async_remote_copy(
        src_ref=sent, dst_ref=cross, send_sem=cross_s, recv_sem=cross_r, device_id=partner, device_id_type=MESH,
    )
    over.start()
    own[...] = jnp.where(core == 0, first, second)
    for p in range(3):
        att[p, far_queries] = pairs[p]
    over.wait()
    sent[...] = (own[...] + cross[...].astype(F32)).astype(BF16)

    for i, j in STEPS:
        ox, oy = lax.rem(x + i, 4), lax.rem(y + j, 4)
        k = owned_by(ox, oy, core)

        @pl.when(k < OWNERS)
        def _():
            pltpu.make_async_remote_copy(
                src_ref=sent.at[pl.ds(pl.multiple_of(k * ROWS, ROWS), ROWS)], dst_ref=part.at[chip],
                send_sem=s1, recv_sem=r1, device_id=device(ox, oy, core, z), device_id_type=MESH,
            ).start()

    loads[4].wait()
    branch = mm(att[0], out_w[0:128]) + mm(att[1], out_w[128:256]) + mm(att[2], out_w[256:384])
    upd_ref[...] = (tok[...].astype(F32) + branch).astype(BF16)

    def total_of(ref, count):
        total = ref[0].astype(F32)
        for i in range(1, count):
            total = total + ref[i].astype(F32)
        return total.astype(BF16)

    @pl.when(owns)
    def _():
        part[chip] = sent[pl.ds(pl.multiple_of(mine * ROWS, ROWS), ROWS)]
        pltpu.make_async_copy(part.at[pl.ds(0, 15)], part.at[pl.ds(0, 15)], r1).wait()
        z1[z] = total_of(part, 16)
        for i in ALONG:
            pltpu.make_async_remote_copy(
                src_ref=z1.at[z], dst_ref=z1.at[z], send_sem=sz1, recv_sem=rz1,
                device_id=device(x, y, core, lax.rem(z + i, 16)), device_id_type=MESH,
            ).start()
        pltpu.make_async_copy(z1.at[pl.ds(0, 15)], z1.at[pl.ds(0, 15)], rz1).wait()
        row = pl.multiple_of(core * HALF + mine * ROWS, ROWS)
        gath[pl.ds(row, ROWS)] = total_of(z1, 16)

        for i, j in STEPS:
            pltpu.make_async_remote_copy(
                src_ref=gath.at[pl.ds(row, ROWS)], dst_ref=gath.at[pl.ds(row, ROWS)], send_sem=s3,
                recv_sem=r3.at[mine], device_id=device(lax.rem(x + i, 4), lax.rem(y + j, 4), core, z), device_id_type=MESH,
            ).start()

    for i, j in ((0, 0),) + tuple(reversed(STEPS)):
        k = owned_by(lax.rem(x + i, 4), lax.rem(y + j, 4), core)

        @pl.when(k < OWNERS)
        def _():
            block = gath.at[pl.ds(pl.multiple_of(core * HALF + k * ROWS, ROWS), ROWS)]
            if i or j:
                pltpu.make_async_copy(block, block, r3.at[k]).wait()
            pltpu.make_async_remote_copy(
                src_ref=block, dst_ref=block, send_sem=s4, recv_sem=r4, device_id=partner, device_id_type=MESH,
            ).start()

    half = gath.at[pl.ds(0, HALF)]
    kept = pl.ds(pl.multiple_of(core * HALF, ROWS), HALF)
    grad_ref[kept] = gath[kept].astype(F32)
    pltpu.make_async_copy(half, half, r4).wait()
    given = pl.ds(pl.multiple_of((1 - core) * HALF, ROWS), HALF)
    grad_ref[given] = gath[given].astype(F32)

    pltpu.make_async_copy(half, half, s4).wait()
    for i, (dr, dc, _, _, _) in enumerate(SENDS):
        @pl.when(there(dr, dc))
        def _():
            halo_copy(i).wait_send()

    @pl.when(owns)
    def _():
        pltpu.make_async_copy(sent.at[pl.ds(0, HALF - ROWS)], sent.at[pl.ds(0, HALF - ROWS)], s1).wait()
        pltpu.make_async_copy(z1.at[pl.ds(0, 15)], z1.at[pl.ds(0, 15)], sz1).wait()
        pltpu.make_async_copy(part.at[pl.ds(0, 15)], part.at[pl.ds(0, 15)], s3).wait()

    @pl.when(jnp.logical_not(owns))
    def _():
        pltpu.make_async_copy(sent, sent, s1).wait()


def hand_over(upd_ref, grad_ref, upd_hbm, grad_hbm, sems):
    copies = [
        pltpu.make_async_copy(grad_ref, grad_hbm, sems.at[0]),
        pltpu.make_async_copy(upd_ref, upd_hbm, sems.at[1]),
    ]
    for copy in copies:
        copy.start()
    for copy in copies:
        copy.wait()


def body(tokens, timesteps, cond_weight, qkv_weight, head_scale, out_weight, cotangent):
    anywhere = pl.BlockSpec(memory_space=pltpu.HBM)
    whole = pl.BlockSpec(memory_space=pltpu.VMEM)
    dma = pltpu.SemaphoreType.DMA
    updated, grad = pl.pallas_call(
        kernel,
        out_shape=(pltpu.VMEM((TOKENS, CH), BF16), pltpu.VMEM((CH, CH), F32)),
        in_specs=[anywhere] * 6 + [pl.BlockSpec(memory_space=pltpu.SMEM)],
        out_specs=(whole, whole),
        scratch_shapes=[
            pltpu.VMEM((TOKENS, CH), BF16),
            pltpu.VMEM((TOKENS, CH), BF16),
            pltpu.VMEM((CH, 3 * CH), BF16),
            pltpu.VMEM((CH, CH), BF16),
            pltpu.VMEM((256, CH), BF16),
            pltpu.SMEM((6,), F32),
            pltpu.VMEM((160, CH), BF16),
            pltpu.VMEM((HALO, CH), BF16),
            pltpu.VMEM((3, 2, TOKENS, 128), BF16),
            pltpu.VMEM((3, 2, TOKENS + HALO, 128), BF16),
            pltpu.VMEM((3, TOKENS + HALO, 256), BF16),
            pltpu.VMEM((3, 2, TOKENS, 256), F32),
            pltpu.VMEM((3, TOKENS, 128), BF16),
            pltpu.VMEM((3, 128, CH), F32),
            pltpu.VMEM((HALF, CH), F32),
            pltpu.VMEM((HALF, CH), BF16),
            pltpu.VMEM((HALF, CH), BF16),
            pltpu.VMEM((16, ROWS, CH), BF16),
            pltpu.VMEM((16, ROWS, CH), BF16),
            pltpu.VMEM((CH, CH), BF16),
            dma((6,)), dma(()), dma((8,)),
        ] + [dma(())] * 7 + [dma((OWNERS,)), dma(()), dma(())],
        compiler_params=pltpu.CompilerParams(collective_id=0, has_side_effects=True, vmem_limit_bytes=40 * 2**20),
    )(*(
        pltpu.with_memory_space_constraint(array, pltpu.HBM)
        for array in (
            tokens.reshape(TOKENS, CH), cotangent.reshape(TOKENS, CH),
            qkv_weight, out_weight, cond_weight, head_scale,
        )
    ), timesteps)
    updated, grad = pl.pallas_call(
        hand_over,
        out_shape=(pltpu.HBM((TOKENS, CH), BF16), pltpu.HBM((CH, CH), F32)),
        in_specs=[pl.BlockSpec(memory_space=pl.ANY)] * 2,
        out_specs=(pl.BlockSpec(memory_space=pl.ANY),) * 2,
        scratch_shapes=[dma((2,))],
    )(pltpu.with_memory_space_constraint(updated, pltpu.VMEM), pltpu.with_memory_space_constraint(grad, pltpu.VMEM))
    return updated.reshape(tokens.shape), grad


def solution(mesh):
    return jax.shard_map(
        body,
        mesh=mesh,
        in_specs=(
            P("dp", "tile", None, None, None),
            P("dp"),
            P(),
            P(),
            P(),
            P(),
            P("dp", "tile", None, None, None),
        ),
        out_specs=(P("dp", "tile", None, None, None), P()),
        check_vma=False,
    )
```

```python
import math

import jax
import jax.numpy as jnp
from jax import lax
from jax.experimental import pallas as pl
from jax.experimental.pallas import tpu as pltpu
from jax.sharding import PartitionSpec as P

MESH = pl.DeviceIdType.MESH
F32, BF16 = jnp.float32, jnp.bfloat16
TOKENS = 256
CH = 384
HALO = 384
PART = 128
STRIP = 48
ROWS = 16
OWNERS = 12
HALF = OWNERS * ROWS
FAR = -16384.0
SENDS = (
    (1, 0, 208, 48, 0),
    (-1, 0, 0, 48, 128),
    (1, 1, 96, 16, 48),
    (1, -1, 112, 16, 64),
    (-1, 1, 128, 16, 176),
    (-1, -1, 144, 16, 192),
    (0, 1, 0, 48, 256),
    (0, -1, 48, 48, 304),
)

STEPS = sorted(
    ((i, j) for i in range(4) for j in range(4) if i or j), key=lambda s: (-min(s[0], 4 - s[0]) - min(s[1], 4 - s[1]), s)
)

ALONG = sorted(range(1, 16), key=lambda i: -min(i, 16 - i))


def mm(a, b):
    return jnp.dot(a, b, preferred_element_type=F32)


def iota(shape, axis):
    return lax.broadcasted_iota(jnp.int32, shape, axis)


def thirds(m):
    return (m >= 3).astype(jnp.int32) + (m >= 6).astype(jnp.int32) + (m >= 9).astype(jnp.int32)


def pick_matrix():
    r = iota((160, TOKENS), 0)
    m48 = jnp.where(r >= 48, r - 48, r)
    side = (m48 % 16) * 16 + m48 // 16 + jnp.where(r < 48, 13, 0)
    m = r % 16
    third = thirds(m)
    corner = third * 16 + m - 3 * third + jnp.where(r < 128, 13 * 16, 0)
    corner = corner + jnp.where((r < 112) | ((r >= 128) & (r < 144)), 13, 0)
    corner = jnp.where(m < 9, corner, -1)
    wanted = jnp.where(r < 96, side, corner)
    return jnp.where(iota((160, TOKENS), 1) == wanted, 1.0, 0.0).astype(BF16)


def key_marks(kr, kc, known, base):
    f = iota(kr.shape, 1) - base
    apart = jnp.where(f < 16, jnp.abs(kr - f), jnp.abs(kc - (f - 16)))
    bad = (apart > 3) | jnp.logical_not(known)
    return jnp.where(bad & (f >= 0) & (f < 32), FAR, 0.0)


def own_places(shape):
    i = iota(shape, 0)
    return i // 16, i % 16


def side_places(grid_col):
    j = iota((PART, 128), 0)
    west = j < 48
    m = jnp.where(west, j, j - 48)
    known = (j < 96) & ((west & (grid_col > 0)) | (jnp.logical_not(west) & (grid_col < 3)))
    return m % 16, m // 16 + jnp.where(west, -3, 16), known


def strip_places(top, grid_row, grid_col):
    j = iota((PART, 128), 0)
    c = j % 16
    third = thirds(c)
    corner, west = j >= 48, j < 64
    kr = jnp.where(corner, third, j // 16) + jnp.where(top, -3, 16)
    kc = jnp.where(corner, c - 3 * third + jnp.where(west, -3, 16), c)
    known = (west & (grid_col > 0)) | (jnp.logical_not(west) & (grid_col < 3))
    known = jnp.logical_not(corner) | (known & (c < 9) & (j < 80))
    beyond = jnp.where(top, grid_row > 0, grid_row < 3)
    return kr, kc, known & beyond


def device(x, y, core, z):
    return (x * 8 + lax.rem(z, 8), (z // 8) * 8 + y * 2 + core)


def owned_by(x, y, core):
    y = jnp.where(core == 0, y, 3 - y)
    return jnp.where(x == y, OWNERS, x * 3 + y - jnp.where(y > x, 1, 0))


def kernel(
    tok_hbm, cot_hbm, qkv_hbm, out_w_hbm, cond_hbm, scale_hbm, step_ref,
    upd_ref, grad_ref,
    tok, cot, qkv, out_w, cond, scale_ref, packed, halo, q_s, k_s, v_s, acc, att, early,
    own, cross, sent, part, z1, gath,
    in_sem, halo_s, halo_r, cross_s, cross_r, s1, r1, sz1, rz1, s3, r3, s4, r4,
):
    dp, tile = lax.axis_index("dp"), lax.axis_index("tile")
    grid_row, grid_col = tile // 4, lax.rem(tile, 4)
    x, z = dp // 8, (tile // 8) * 8 + lax.rem(dp, 8)
    y, core = lax.rem(tile, 8) // 2, lax.rem(tile, 2)
    chip = x * 4 + y
    mine = owned_by(x, y, core)
    owns = mine < OWNERS
    partner = (dp, tile + 1 - 2 * core)

    loads = [
        pltpu.make_async_copy(src, dst, in_sem.at[i])
        for i, (src, dst) in enumerate(((tok_hbm, tok), (cond_hbm, cond), (qkv_hbm, qkv), (cot_hbm, cot), (out_w_hbm, out_w), (scale_hbm, scale_ref)))
    ]
    halo[...] = jnp.zeros_like(halo)
    barrier = pltpu.get_barrier_semaphore()

    def there(dr, dc):
        ok = True
        if dr:
            ok = (grid_row < 3) if dr > 0 else (grid_row > 0)
        if dc:
            right = (grid_col < 3) if dc > 0 else (grid_col > 0)
            ok = (ok & right) if dr else right
        return ok

    near = 0
    for dr, dc, _, _, _ in SENDS:
        ok = there(dr, dc)
        near = near + jnp.where(ok, 1, 0)

        @pl.when(ok)
        def _():
            pl.semaphore_signal(barrier, inc=1, device_id=(dp, tile + 4 * dr + dc), device_id_type=MESH)

    for load in loads:
        load.start()
    pl.semaphore_signal(barrier, inc=1, device_id=partner, device_id_type=MESH)
    for i in ALONG:
        pl.semaphore_signal(barrier, inc=1, device_id=device(x, y, core, lax.rem(z + i, 16)), device_id_type=MESH)
    for i, j in STEPS:
        pl.semaphore_signal(barrier, inc=1, device_id=device(lax.rem(x + i, 4), lax.rem(y + j, 4), core, z), device_id_type=MESH)

    loads[0].wait()
    packed[...] = mm(pick_matrix(), tok[...]).astype(BF16)

    pl.semaphore_wait(barrier, 31 + near)

    def halo_copy(i):
        dr, dc, place, count, into = SENDS[i]
        source = tok if dc == 0 else packed
        return pltpu.make_async_remote_copy(
            src_ref=source.at[pl.ds(place, count)], dst_ref=halo.at[pl.ds(into, count)],
            send_sem=halo_s, recv_sem=halo_r.at[i], device_id=(dp, tile + 4 * dr + dc), device_id_type=MESH,
        )

    for i, (dr, dc, _, _, _) in enumerate(SENDS):
        @pl.when(there(dr, dc))
        def _():
            halo_copy(i).start()

    loads[1].wait()
    loads[5].wait()
    frequency = jnp.exp((-math.log(10000.0) / 128) * iota((8, 128), 1).astype(F32))
    angles = step_ref[0].astype(F32) * frequency
    features = jnp.concatenate([jnp.cos(angles), jnp.sin(angles)], axis=1)
    high = features.astype(BF16)
    rest = features - high.astype(F32)
    middle = rest.astype(BF16)
    low = (rest - middle.astype(F32)).astype(BF16)
    gain = 1.0 + mm(high, cond[...]) + mm(middle, cond[...]) + mm(low, cond[...])
    gain = gain[0:1]

    same_head = jnp.where((iota((128, 128), 0) < 64) == (iota((128, 128), 1) < 64), 1.0, 0.0).astype(BF16)
    same_head = jnp.concatenate([same_head, same_head], axis=0)

    def normed(rows):
        wide = rows.astype(F32)
        mean_square = jnp.mean(wide * wide, axis=-1, keepdims=True)
        return (wide * lax.rsqrt(mean_square + 1e-06) * gain).astype(BF16)

    def units(wide):
        count = wide.shape[0]
        pairs = jnp.concatenate([wide[:, 128 * p:128 * (p + 1)] for p in range(3)], axis=0)
        square = pairs * pairs
        high = square.astype(BF16)
        low = (square - high.astype(F32)).astype(BF16)
        total = mm(jnp.concatenate([high, low], axis=1), same_head)
        pairs = pairs * lax.rsqrt(total + 1e-06)
        return [pairs[count * p:count * (p + 1)] for p in range(3)]

    def left_of(count):
        return iota((count, 128), 1) < 64

    def put_keys(rows, begin, places):
        count = rows.shape[0]
        where, left = slice(begin, begin + count), left_of(count)
        even, odd = key_marks(*places, 64), key_marks(*places, 0)
        both = mm(rows, qkv[:, CH:3 * CH])
        keys = units(both[:, :CH])
        for p in range(3):
            k_s[p, 0, where] = jnp.where(left, keys[p], even).astype(BF16)
            k_s[p, 1, where] = jnp.where(left, odd, keys[p]).astype(BF16)
            v_s[p, where, 0:128] = both[:, CH + 128 * p:CH + 128 * (p + 1)].astype(BF16)

    def attend(p, e, queries, begin, count):
        keys = slice(begin, begin + count)
        score = lax.dot_general(q_s[p, e, queries], k_s[p, e, keys], (((1,), (1,)), ((), ())), preferred_element_type=F32)
        return mm(jnp.exp2(score).astype(BF16), v_s[p, keys])

    def shares(r0, r1):
        left = left_of(r0.shape[0])
        return jnp.where(left, r0[:, :128] / r0[:, 128:], r1[:, :128] / r1[:, 128:]).astype(BF16)

    def outer(rows, cots):
        return lax.dot_general(rows, cots, (((0,), (0,)), ((), ())), preferred_element_type=F32)

    def await_halo(steps, wanted):
        for i, (dr, dc, _, _, _) in enumerate(SENDS):
            if dr not in steps:
                continue

            @pl.when(there(-dr, -dc) & wanted(dr))
            def _():
                halo_copy(i).wait_recv()

    loads[2].wait()
    rows = normed(tok[...])
    kr, kc = own_places((TOKENS, 128))
    f = iota((TOKENS, 128), 1)

    def query_marks(base):
        g = f - base
        hit = ((g >= 0) & (g < 16) & (g == kr)) | ((g >= 16) & (g < 32) & (g - 16 == kc))
        return jnp.where(hit, 1.0, 0.0)

    even, odd = query_marks(64), query_marks(0)
    left = left_of(TOKENS)
    v_s[:, :, 128:256] = jnp.ones((3, TOKENS + HALO, 128), BF16)
    queries = units(mm(rows, qkv[:, 0:CH]))
    for p in range(3):
        scales = jnp.where(left, scale_ref[2 * p], scale_ref[2 * p + 1]) * math.log2(math.e)
        query = queries[p] * scales
        q_s[p, 0] = jnp.where(left, query, even).astype(BF16)
        q_s[p, 1] = jnp.where(left, odd, query).astype(BF16)
    put_keys(rows, 0, (kr, kc, kr >= 0))
    every = slice(0, TOKENS)
    for p in range(3):
        for e in range(2):
            acc[p, e] = attend(p, e, every, 0, TOKENS)

    await_halo((0,), lambda dr: True)
    put_keys(normed(halo[2 * PART:3 * PART]), TOKENS, side_places(grid_col))
    for p in range(3):
        for e in range(2):
            acc[p, e] += attend(p, e, every, TOKENS, PART)

    top_last = lax.rem(grid_row, 2) == 0
    await_halo((-1, 1), lambda dr: top_last if dr < 0 else jnp.logical_not(top_last))
    near_rows = pl.multiple_of(jnp.where(top_last, PART, 0), PART)
    put_keys(normed(halo[pl.ds(near_rows, PART)]), TOKENS + PART, strip_places(jnp.logical_not(top_last), grid_row, grid_col))
    near_queries = pl.ds(pl.multiple_of(jnp.where(top_last, TOKENS - STRIP, 0), 16), STRIP)
    for p in range(3):
        for e in range(2):
            acc[p, e, near_queries] += attend(p, e, near_queries, TOKENS + PART, PART)

    loads[3].wait()
    done = pl.ds(pl.multiple_of(jnp.where(top_last, STRIP, 0), 16), TOKENS - STRIP)
    for p in range(3):
        att[p] = shares(acc[p, 0], acc[p, 1])
        early[p] = outer(att[p, done], cot[done])

    far_rows = pl.multiple_of(jnp.where(top_last, 0, PART), PART)
    far_queries = pl.ds(pl.multiple_of(jnp.where(top_last, 0, TOKENS - STRIP), 16), STRIP)
    places = strip_places(top_last, grid_row, grid_col)
    await_halo((-1, 1), lambda dr: jnp.logical_not(top_last) if dr < 0 else top_last)
    put_keys(normed(halo[pl.ds(far_rows, PART)]), TOKENS + 2 * PART, places)
    late = [
        [acc[p, e, far_queries] + attend(p, e, far_queries, TOKENS + 2 * PART, PART) for e in range(2)] for p in range(3)
    ]
    pairs = [shares(*r) for r in late]
    far_cot = cot[far_queries]
    grads = [early[p] + outer(pairs[p], far_cot) for p in range(3)]
    first = jnp.concatenate([grads[0], grads[1][0:64]], axis=0)
    second = jnp.concatenate([grads[1][64:128], grads[2]], axis=0)
    sent[...] = jnp.where(core == 0, second, first).astype(BF16)
    over = pltpu.make_async_remote_copy(
        src_ref=sent, dst_ref=cross, send_sem=cross_s, recv_sem=cross_r, device_id=partner, device_id_type=MESH,
    )
    over.start()
    own[...] = jnp.where(core == 0, first, second)
    for p in range(3):
        att[p, far_queries] = pairs[p]
    over.wait()
    sent[...] = (own[...] + cross[...].astype(F32)).astype(BF16)

    for i, j in STEPS:
        ox, oy = lax.rem(x + i, 4), lax.rem(y + j, 4)
        k = owned_by(ox, oy, core)

        @pl.when(k < OWNERS)
        def _():
            pltpu.make_async_remote_copy(
                src_ref=sent.at[pl.ds(pl.multiple_of(k * ROWS, ROWS), ROWS)], dst_ref=part.at[chip],
                send_sem=s1, recv_sem=r1, device_id=device(ox, oy, core, z), device_id_type=MESH,
            ).start()

    loads[4].wait()
    branch = mm(att[0], out_w[0:128]) + mm(att[1], out_w[128:256]) + mm(att[2], out_w[256:384])
    upd_ref[...] = (tok[...].astype(F32) + branch).astype(BF16)

    def total_of(ref, count):
        total = ref[0].astype(F32)
        for i in range(1, count):
            total = total + ref[i].astype(F32)
        return total.astype(BF16)

    @pl.when(owns)
    def _():
        part[chip] = sent[pl.ds(pl.multiple_of(mine * ROWS, ROWS), ROWS)]
        pltpu.make_async_copy(part.at[pl.ds(0, 15)], part.at[pl.ds(0, 15)], r1).wait()
        z1[z] = total_of(part, 16)
        for i in ALONG:
            pltpu.make_async_remote_copy(
                src_ref=z1.at[z], dst_ref=z1.at[z], send_sem=sz1, recv_sem=rz1,
                device_id=device(x, y, core, lax.rem(z + i, 16)), device_id_type=MESH,
            ).start()
        pltpu.make_async_copy(z1.at[pl.ds(0, 15)], z1.at[pl.ds(0, 15)], rz1).wait()
        row = pl.multiple_of(core * HALF + mine * ROWS, ROWS)
        gath[pl.ds(row, ROWS)] = total_of(z1, 16)

        for i, j in STEPS:
            pltpu.make_async_remote_copy(
                src_ref=gath.at[pl.ds(row, ROWS)], dst_ref=gath.at[pl.ds(row, ROWS)], send_sem=s3,
                recv_sem=r3.at[mine], device_id=device(lax.rem(x + i, 4), lax.rem(y + j, 4), core, z), device_id_type=MESH,
            ).start()

    for i, j in ((0, 0),) + tuple(reversed(STEPS)):
        k = owned_by(lax.rem(x + i, 4), lax.rem(y + j, 4), core)

        @pl.when(k < OWNERS)
        def _():
            block = gath.at[pl.ds(pl.multiple_of(core * HALF + k * ROWS, ROWS), ROWS)]
            if i or j:
                pltpu.make_async_copy(block, block, r3.at[k]).wait()
            pltpu.make_async_remote_copy(
                src_ref=block, dst_ref=block, send_sem=s4, recv_sem=r4, device_id=partner, device_id_type=MESH,
            ).start()

    half = gath.at[pl.ds(0, HALF)]
    kept = pl.ds(pl.multiple_of(core * HALF, ROWS), HALF)
    grad_ref[kept] = gath[kept].astype(F32)
    pltpu.make_async_copy(half, half, r4).wait()
    given = pl.ds(pl.multiple_of((1 - core) * HALF, ROWS), HALF)
    grad_ref[given] = gath[given].astype(F32)

    pltpu.make_async_copy(half, half, s4).wait()
    for i, (dr, dc, _, _, _) in enumerate(SENDS):
        @pl.when(there(dr, dc))
        def _():
            halo_copy(i).wait_send()

    @pl.when(owns)
    def _():
        pltpu.make_async_copy(sent.at[pl.ds(0, HALF - ROWS)], sent.at[pl.ds(0, HALF - ROWS)], s1).wait()
        pltpu.make_async_copy(z1.at[pl.ds(0, 15)], z1.at[pl.ds(0, 15)], sz1).wait()
        pltpu.make_async_copy(part.at[pl.ds(0, 15)], part.at[pl.ds(0, 15)], s3).wait()

    @pl.when(jnp.logical_not(owns))
    def _():
        pltpu.make_async_copy(sent, sent, s1).wait()


def hand_over(upd_ref, grad_ref, upd_hbm, grad_hbm, sems):
    copies = [
        pltpu.make_async_copy(grad_ref, grad_hbm, sems.at[0]),
        pltpu.make_async_copy(upd_ref, upd_hbm, sems.at[1]),
    ]
    for copy in copies:
        copy.start()
    for copy in copies:
        copy.wait()


def body(tokens, timesteps, cond_weight, qkv_weight, head_scale, out_weight, cotangent):
    anywhere = pl.BlockSpec(memory_space=pltpu.HBM)
    whole = pl.BlockSpec(memory_space=pltpu.VMEM)
    dma = pltpu.SemaphoreType.DMA
    updated, grad = pl.pallas_call(
        kernel,
        out_shape=(pltpu.VMEM((TOKENS, CH), BF16), pltpu.VMEM((CH, CH), F32)),
        in_specs=[anywhere] * 6 + [pl.BlockSpec(memory_space=pltpu.SMEM)],
        out_specs=(whole, whole),
        scratch_shapes=[
            pltpu.VMEM((TOKENS, CH), BF16),
            pltpu.VMEM((TOKENS, CH), BF16),
            pltpu.VMEM((CH, 3 * CH), BF16),
            pltpu.VMEM((CH, CH), BF16),
            pltpu.VMEM((256, CH), BF16),
            pltpu.SMEM((6,), F32),
            pltpu.VMEM((160, CH), BF16),
            pltpu.VMEM((HALO, CH), BF16),
            pltpu.VMEM((3, 2, TOKENS, 128), BF16),
            pltpu.VMEM((3, 2, TOKENS + HALO, 128), BF16),
            pltpu.VMEM((3, TOKENS + HALO, 256), BF16),
            pltpu.VMEM((3, 2, TOKENS, 256), F32),
            pltpu.VMEM((3, TOKENS, 128), BF16),
            pltpu.VMEM((3, 128, CH), F32),
            pltpu.VMEM((HALF, CH), F32),
            pltpu.VMEM((HALF, CH), BF16),
            pltpu.VMEM((HALF, CH), BF16),
            pltpu.VMEM((16, ROWS, CH), BF16),
            pltpu.VMEM((16, ROWS, CH), BF16),
            pltpu.VMEM((CH, CH), BF16),
            dma((6,)), dma(()), dma((8,)),
        ] + [dma(())] * 7 + [dma((OWNERS,)), dma(()), dma(())],
        compiler_params=pltpu.CompilerParams(collective_id=0, has_side_effects=True, vmem_limit_bytes=40 * 2**20),
    )(*(
        pltpu.with_memory_space_constraint(array, pltpu.HBM)
        for array in (
            tokens.reshape(TOKENS, CH), cotangent.reshape(TOKENS, CH),
            qkv_weight, out_weight, cond_weight, head_scale,
        )
    ), timesteps)
    updated, grad = pl.pallas_call(
        hand_over,
        out_shape=(pltpu.HBM((TOKENS, CH), BF16), pltpu.HBM((CH, CH), F32)),
        in_specs=[pl.BlockSpec(memory_space=pl.ANY)] * 2,
        out_specs=(pl.BlockSpec(memory_space=pl.ANY),) * 2,
        scratch_shapes=[dma((2,))],
    )(pltpu.with_memory_space_constraint(updated, pltpu.VMEM), pltpu.with_memory_space_constraint(grad, pltpu.VMEM))
    return updated.reshape(tokens.shape), grad


def solution(mesh):
    return jax.shard_map(
        body,
        mesh=mesh,
        in_specs=(
            P("dp", "tile", None, None, None),
            P("dp"),
            P(),
            P(),
            P(),
            P(),
            P("dp", "tile", None, None, None),
        ),
        out_specs=(P("dp", "tile", None, None, None), P()),
        check_vma=False,
    )
```

```python
import math

import jax
import jax.numpy as jnp
from jax import lax
from jax.experimental import pallas as pl
from jax.experimental.pallas import tpu as pltpu
from jax.sharding import PartitionSpec as P

MESH = pl.DeviceIdType.MESH
F32, BF16 = jnp.float32, jnp.bfloat16
TOKENS = 256
CH = 384
HALO = 384
PART = 128
STRIP = 48
ROWS = 16
OWNERS = 12
HALF = OWNERS * ROWS
FAR = -16384.0
SENDS = (
    (1, 0, 208, 48, 0),
    (-1, 0, 0, 48, 128),
    (1, 1, 96, 16, 48),
    (1, -1, 112, 16, 64),
    (-1, 1, 128, 16, 176),
    (-1, -1, 144, 16, 192),
    (0, 1, 0, 48, 256),
    (0, -1, 48, 48, 304),
)

STEPS = sorted(
    ((i, j) for i in range(4) for j in range(4) if i or j), key=lambda s: (-min(s[0], 4 - s[0]) - min(s[1], 4 - s[1]), s)
)

ALONG = sorted(range(1, 16), key=lambda i: -min(i, 16 - i))


def mm(a, b):
    return jnp.dot(a, b, preferred_element_type=F32)


def iota(shape, axis):
    return lax.broadcasted_iota(jnp.int32, shape, axis)


def thirds(m):
    return (m >= 3).astype(jnp.int32) + (m >= 6).astype(jnp.int32) + (m >= 9).astype(jnp.int32)


def pick_matrix():
    r = iota((160, TOKENS), 0)
    m48 = jnp.where(r >= 48, r - 48, r)
    side = (m48 % 16) * 16 + m48 // 16 + jnp.where(r < 48, 13, 0)
    m = r % 16
    third = thirds(m)
    corner = third * 16 + m - 3 * third + jnp.where(r < 128, 13 * 16, 0)
    corner = corner + jnp.where((r < 112) | ((r >= 128) & (r < 144)), 13, 0)
    corner = jnp.where(m < 9, corner, -1)
    wanted = jnp.where(r < 96, side, corner)
    return jnp.where(iota((160, TOKENS), 1) == wanted, 1.0, 0.0).astype(BF16)


def key_marks(kr, kc, known, base):
    f = iota(kr.shape, 1) - base
    apart = jnp.where(f < 16, jnp.abs(kr - f), jnp.abs(kc - (f - 16)))
    bad = (apart > 3) | jnp.logical_not(known)
    return jnp.where(bad & (f >= 0) & (f < 32), FAR, 0.0)


def own_places(shape):
    i = iota(shape, 0)
    return i // 16, i % 16


def side_places(grid_col):
    j = iota((PART, 128), 0)
    west = j < 48
    m = jnp.where(west, j, j - 48)
    known = (j < 96) & ((west & (grid_col > 0)) | (jnp.logical_not(west) & (grid_col < 3)))
    return m % 16, m // 16 + jnp.where(west, -3, 16), known


def strip_places(top, grid_row, grid_col):
    j = iota((PART, 128), 0)
    c = j % 16
    third = thirds(c)
    corner, west = j >= 48, j < 64
    kr = jnp.where(corner, third, j // 16) + jnp.where(top, -3, 16)
    kc = jnp.where(corner, c - 3 * third + jnp.where(west, -3, 16), c)
    known = (west & (grid_col > 0)) | (jnp.logical_not(west) & (grid_col < 3))
    known = jnp.logical_not(corner) | (known & (c < 9) & (j < 80))
    beyond = jnp.where(top, grid_row > 0, grid_row < 3)
    return kr, kc, known & beyond


def device(x, y, core, z):
    return (x * 8 + lax.rem(z, 8), (z // 8) * 8 + y * 2 + core)


def owned_by(x, y, core):
    y = jnp.where(core == 0, y, 3 - y)
    return jnp.where(x == y, OWNERS, x * 3 + y - jnp.where(y > x, 1, 0))


def kernel(
    tok_hbm, cot_hbm, qkv_hbm, out_w_hbm, cond_hbm, scale_hbm, step_ref,
    upd_ref, grad_ref,
    tok, cot, qkv, out_w, cond, scale_ref, packed, halo, q_s, k_s, v_s, acc, att, early,
    own, cross, sent, summed, part, z1, gath,
    in_sem, halo_s, halo_r, cross_s, cross_r, s1, r1, sz1, rz1, s3, r3, s4, r4,
):
    dp, tile = lax.axis_index("dp"), lax.axis_index("tile")
    grid_row, grid_col = tile // 4, lax.rem(tile, 4)
    x, z = dp // 8, (tile // 8) * 8 + lax.rem(dp, 8)
    y, core = lax.rem(tile, 8) // 2, lax.rem(tile, 2)
    chip = x * 4 + y
    mine = owned_by(x, y, core)
    owns = mine < OWNERS
    partner = (dp, tile + 1 - 2 * core)

    loads = [
        pltpu.make_async_copy(src, dst, in_sem.at[i])
        for i, (src, dst) in enumerate(((tok_hbm, tok), (cond_hbm, cond), (qkv_hbm, qkv), (cot_hbm, cot), (out_w_hbm, out_w), (scale_hbm, scale_ref)))
    ]
    halo[...] = jnp.zeros_like(halo)
    barrier = pltpu.get_barrier_semaphore()

    def there(dr, dc):
        ok = True
        if dr:
            ok = (grid_row < 3) if dr > 0 else (grid_row > 0)
        if dc:
            right = (grid_col < 3) if dc > 0 else (grid_col > 0)
            ok = (ok & right) if dr else right
        return ok

    near = 0
    for dr, dc, _, _, _ in SENDS:
        ok = there(dr, dc)
        near = near + jnp.where(ok, 1, 0)

        @pl.when(ok)
        def _():
            pl.semaphore_signal(barrier, inc=1, device_id=(dp, tile + 4 * dr + dc), device_id_type=MESH)

    for load in loads:
        load.start()
    pl.semaphore_signal(barrier, inc=1, device_id=partner, device_id_type=MESH)
    for i in ALONG:
        pl.semaphore_signal(barrier, inc=1, device_id=device(x, y, core, lax.rem(z + i, 16)), device_id_type=MESH)
    for i, j in STEPS:
        pl.semaphore_signal(barrier, inc=1, device_id=device(lax.rem(x + i, 4), lax.rem(y + j, 4), core, z), device_id_type=MESH)

    loads[0].wait()
    packed[...] = mm(pick_matrix(), tok[...]).astype(BF16)

    pl.semaphore_wait(barrier, 31 + near)

    def halo_copy(i):
        dr, dc, place, count, into = SENDS[i]
        source = tok if dc == 0 else packed
        return pltpu.make_async_remote_copy(
            src_ref=source.at[pl.ds(place, count)], dst_ref=halo.at[pl.ds(into, count)],
            send_sem=halo_s, recv_sem=halo_r.at[i], device_id=(dp, tile + 4 * dr + dc), device_id_type=MESH,
        )

    for i, (dr, dc, _, _, _) in enumerate(SENDS):
        @pl.when(there(dr, dc))
        def _():
            halo_copy(i).start()

    loads[1].wait()
    loads[5].wait()
    frequency = jnp.exp((-math.log(10000.0) / 128) * iota((8, 128), 1).astype(F32))
    angles = step_ref[0].astype(F32) * frequency
    features = jnp.concatenate([jnp.cos(angles), jnp.sin(angles)], axis=1)
    high = features.astype(BF16)
    rest = features - high.astype(F32)
    middle = rest.astype(BF16)
    low = (rest - middle.astype(F32)).astype(BF16)
    gain = 1.0 + mm(high, cond[...]) + mm(middle, cond[...]) + mm(low, cond[...])
    gain = gain[0:1]

    same_head = jnp.where((iota((128, 128), 0) < 64) == (iota((128, 128), 1) < 64), 1.0, 0.0).astype(BF16)
    same_head = jnp.concatenate([same_head, same_head], axis=0)

    def normed(rows):
        wide = rows.astype(F32)
        mean_square = jnp.mean(wide * wide, axis=-1, keepdims=True)
        return (wide * lax.rsqrt(mean_square + 1e-06) * gain).astype(BF16)

    def units(wide):
        count = wide.shape[0]
        pairs = jnp.concatenate([wide[:, 128 * p:128 * (p + 1)] for p in range(3)], axis=0)
        square = pairs * pairs
        high = square.astype(BF16)
        low = (square - high.astype(F32)).astype(BF16)
        total = mm(jnp.concatenate([high, low], axis=1), same_head)
        pairs = pairs * lax.rsqrt(total + 1e-06)
        return [pairs[count * p:count * (p + 1)] for p in range(3)]

    def left_of(count):
        return iota((count, 128), 1) < 64

    def put_keys(rows, begin, places):
        count = rows.shape[0]
        where, left = slice(begin, begin + count), left_of(count)
        even, odd = key_marks(*places, 64), key_marks(*places, 0)
        both = mm(rows, qkv[:, CH:3 * CH])
        keys = units(both[:, :CH])
        for p in range(3):
            k_s[p, 0, where] = jnp.where(left, keys[p], even).astype(BF16)
            k_s[p, 1, where] = jnp.where(left, odd, keys[p]).astype(BF16)
            v_s[p, where, 0:128] = both[:, CH + 128 * p:CH + 128 * (p + 1)].astype(BF16)

    def attend(p, e, queries, begin, count):
        keys = slice(begin, begin + count)
        score = lax.dot_general(q_s[p, e, queries], k_s[p, e, keys], (((1,), (1,)), ((), ())), preferred_element_type=F32)
        return mm(jnp.exp2(score).astype(BF16), v_s[p, keys])

    def shares(r0, r1):
        left = left_of(r0.shape[0])
        return jnp.where(left, r0[:, :128] / r0[:, 128:], r1[:, :128] / r1[:, 128:]).astype(BF16)

    def outer(rows, cots):
        return lax.dot_general(rows, cots, (((0,), (0,)), ((), ())), preferred_element_type=F32)

    def await_halo(steps, wanted):
        for i, (dr, dc, _, _, _) in enumerate(SENDS):
            if dr not in steps:
                continue

            @pl.when(there(-dr, -dc) & wanted(dr))
            def _():
                halo_copy(i).wait_recv()

    loads[2].wait()
    rows = normed(tok[...])
    kr, kc = own_places((TOKENS, 128))
    f = iota((TOKENS, 128), 1)

    def query_marks(base):
        g = f - base
        hit = ((g >= 0) & (g < 16) & (g == kr)) | ((g >= 16) & (g < 32) & (g - 16 == kc))
        return jnp.where(hit, 1.0, 0.0)

    even, odd = query_marks(64), query_marks(0)
    left = left_of(TOKENS)
    v_s[:, :, 128:256] = jnp.ones((3, TOKENS + HALO, 128), BF16)
    queries = units(mm(rows, qkv[:, 0:CH]))
    for p in range(3):
        scales = jnp.where(left, scale_ref[2 * p], scale_ref[2 * p + 1]) * math.log2(math.e)
        query = queries[p] * scales
        q_s[p, 0] = jnp.where(left, query, even).astype(BF16)
        q_s[p, 1] = jnp.where(left, odd, query).astype(BF16)
    put_keys(rows, 0, (kr, kc, kr >= 0))
    every = slice(0, TOKENS)
    for p in range(3):
        for e in range(2):
            acc[p, e] = attend(p, e, every, 0, TOKENS)

    await_halo((0,), lambda dr: True)
    put_keys(normed(halo[2 * PART:3 * PART]), TOKENS, side_places(grid_col))
    for p in range(3):
        for e in range(2):
            acc[p, e] += attend(p, e, every, TOKENS, PART)

    top_last = lax.rem(grid_row, 2) == 0
    await_halo((-1, 1), lambda dr: top_last if dr < 0 else jnp.logical_not(top_last))
    near_rows = pl.multiple_of(jnp.where(top_last, PART, 0), PART)
    put_keys(normed(halo[pl.ds(near_rows, PART)]), TOKENS + PART, strip_places(jnp.logical_not(top_last), grid_row, grid_col))
    near_queries = pl.ds(pl.multiple_of(jnp.where(top_last, TOKENS - STRIP, 0), 16), STRIP)
    for p in range(3):
        for e in range(2):
            acc[p, e, near_queries] += attend(p, e, near_queries, TOKENS + PART, PART)

    loads[3].wait()
    done = pl.ds(pl.multiple_of(jnp.where(top_last, STRIP, 0), 16), TOKENS - STRIP)
    for p in range(3):
        att[p] = shares(acc[p, 0], acc[p, 1])
        early[p] = outer(att[p, done], cot[done])

    far_rows = pl.multiple_of(jnp.where(top_last, 0, PART), PART)
    far_queries = pl.ds(pl.multiple_of(jnp.where(top_last, 0, TOKENS - STRIP), 16), STRIP)
    places = strip_places(top_last, grid_row, grid_col)
    await_halo((-1, 1), lambda dr: jnp.logical_not(top_last) if dr < 0 else top_last)
    put_keys(normed(halo[pl.ds(far_rows, PART)]), TOKENS + 2 * PART, places)
    late = [
        [acc[p, e, far_queries] + attend(p, e, far_queries, TOKENS + 2 * PART, PART) for e in range(2)] for p in range(3)
    ]
    pairs = [shares(*r) for r in late]
    far_cot = cot[far_queries]
    grads = [early[p] + outer(pairs[p], far_cot) for p in range(3)]
    first = jnp.concatenate([grads[0], grads[1][0:64]], axis=0)
    second = jnp.concatenate([grads[1][64:128], grads[2]], axis=0)
    sent[...] = jnp.where(core == 0, second, first).astype(BF16)
    over = []
    for i in range(2):
        piece = pl.ds(i * (HALF // 2), HALF // 2)
        over.append(pltpu.make_async_remote_copy(
            src_ref=sent.at[piece], dst_ref=cross.at[piece], send_sem=cross_s.at[i], recv_sem=cross_r.at[i],
            device_id=partner, device_id_type=MESH,
        ))
        over[i].start()
    own[...] = jnp.where(core == 0, first, second)
    for p in range(3):
        att[p, far_queries] = pairs[p]
    for i in range(2):
        piece = slice(i * (HALF // 2), (i + 1) * (HALF // 2))
        over[i].wait_recv()
        summed[piece] = (own[piece] + cross[piece].astype(F32)).astype(BF16)

    for i, j in STEPS:
        ox, oy = lax.rem(x + i, 4), lax.rem(y + j, 4)
        k = owned_by(ox, oy, core)

        @pl.when(k < OWNERS)
        def _():
            pltpu.make_async_remote_copy(
                src_ref=summed.at[pl.ds(pl.multiple_of(k * ROWS, ROWS), ROWS)], dst_ref=part.at[chip],
                send_sem=s1, recv_sem=r1, device_id=device(ox, oy, core, z), device_id_type=MESH,
            ).start()

    loads[4].wait()
    branch = mm(att[0], out_w[0:128]) + mm(att[1], out_w[128:256]) + mm(att[2], out_w[256:384])
    upd_ref[...] = (tok[...].astype(F32) + branch).astype(BF16)

    def total_of(ref, count):
        total = ref[0].astype(F32)
        for i in range(1, count):
            total = total + ref[i].astype(F32)
        return total.astype(BF16)

    @pl.when(owns)
    def _():
        part[chip] = summed[pl.ds(pl.multiple_of(mine * ROWS, ROWS), ROWS)]
        pltpu.make_async_copy(part.at[pl.ds(0, 15)], part.at[pl.ds(0, 15)], r1).wait()
        z1[z] = total_of(part, 16)
        for i in ALONG:
            pltpu.make_async_remote_copy(
                src_ref=z1.at[z], dst_ref=z1.at[z], send_sem=sz1, recv_sem=rz1,
                device_id=device(x, y, core, lax.rem(z + i, 16)), device_id_type=MESH,
            ).start()
        pltpu.make_async_copy(z1.at[pl.ds(0, 15)], z1.at[pl.ds(0, 15)], rz1).wait()
        row = pl.multiple_of(core * HALF + mine * ROWS, ROWS)
        gath[pl.ds(row, ROWS)] = total_of(z1, 16)

        for i, j in STEPS:
            pltpu.make_async_remote_copy(
                src_ref=gath.at[pl.ds(row, ROWS)], dst_ref=gath.at[pl.ds(row, ROWS)], send_sem=s3,
                recv_sem=r3.at[mine], device_id=device(lax.rem(x + i, 4), lax.rem(y + j, 4), core, z), device_id_type=MESH,
            ).start()

    for i, j in ((0, 0),) + tuple(reversed(STEPS)):
        k = owned_by(lax.rem(x + i, 4), lax.rem(y + j, 4), core)

        @pl.when(k < OWNERS)
        def _():
            block = gath.at[pl.ds(pl.multiple_of(core * HALF + k * ROWS, ROWS), ROWS)]
            if i or j:
                pltpu.make_async_copy(block, block, r3.at[k]).wait()
            pltpu.make_async_remote_copy(
                src_ref=block, dst_ref=block, send_sem=s4, recv_sem=r4, device_id=partner, device_id_type=MESH,
            ).start()

    half = gath.at[pl.ds(0, HALF)]
    kept = pl.ds(pl.multiple_of(core * HALF, ROWS), HALF)
    grad_ref[kept] = gath[kept].astype(F32)
    pltpu.make_async_copy(half, half, r4).wait()
    given = pl.ds(pl.multiple_of((1 - core) * HALF, ROWS), HALF)
    grad_ref[given] = gath[given].astype(F32)

    over[0].wait_send()
    over[1].wait_send()
    pltpu.make_async_copy(half, half, s4).wait()
    for i, (dr, dc, _, _, _) in enumerate(SENDS):
        @pl.when(there(dr, dc))
        def _():
            halo_copy(i).wait_send()

    @pl.when(owns)
    def _():
        pltpu.make_async_copy(summed.at[pl.ds(0, HALF - ROWS)], summed.at[pl.ds(0, HALF - ROWS)], s1).wait()
        pltpu.make_async_copy(z1.at[pl.ds(0, 15)], z1.at[pl.ds(0, 15)], sz1).wait()
        pltpu.make_async_copy(part.at[pl.ds(0, 15)], part.at[pl.ds(0, 15)], s3).wait()

    @pl.when(jnp.logical_not(owns))
    def _():
        pltpu.make_async_copy(summed, summed, s1).wait()


def hand_over(upd_ref, grad_ref, upd_hbm, grad_hbm, sems):
    copies = [
        pltpu.make_async_copy(grad_ref, grad_hbm, sems.at[0]),
        pltpu.make_async_copy(upd_ref, upd_hbm, sems.at[1]),
    ]
    for copy in copies:
        copy.start()
    for copy in copies:
        copy.wait()


def body(tokens, timesteps, cond_weight, qkv_weight, head_scale, out_weight, cotangent):
    anywhere = pl.BlockSpec(memory_space=pltpu.HBM)
    whole = pl.BlockSpec(memory_space=pltpu.VMEM)
    dma = pltpu.SemaphoreType.DMA
    updated, grad = pl.pallas_call(
        kernel,
        out_shape=(pltpu.VMEM((TOKENS, CH), BF16), pltpu.VMEM((CH, CH), F32)),
        in_specs=[anywhere] * 6 + [pl.BlockSpec(memory_space=pltpu.SMEM)],
        out_specs=(whole, whole),
        scratch_shapes=[
            pltpu.VMEM((TOKENS, CH), BF16),
            pltpu.VMEM((TOKENS, CH), BF16),
            pltpu.VMEM((CH, 3 * CH), BF16),
            pltpu.VMEM((CH, CH), BF16),
            pltpu.VMEM((256, CH), BF16),
            pltpu.SMEM((6,), F32),
            pltpu.VMEM((160, CH), BF16),
            pltpu.VMEM((HALO, CH), BF16),
            pltpu.VMEM((3, 2, TOKENS, 128), BF16),
            pltpu.VMEM((3, 2, TOKENS + HALO, 128), BF16),
            pltpu.VMEM((3, TOKENS + HALO, 256), BF16),
            pltpu.VMEM((3, 2, TOKENS, 256), F32),
            pltpu.VMEM((3, TOKENS, 128), BF16),
            pltpu.VMEM((3, 128, CH), F32),
            pltpu.VMEM((HALF, CH), F32),
            pltpu.VMEM((HALF, CH), BF16),
            pltpu.VMEM((HALF, CH), BF16),
            pltpu.VMEM((HALF, CH), BF16),
            pltpu.VMEM((16, ROWS, CH), BF16),
            pltpu.VMEM((16, ROWS, CH), BF16),
            pltpu.VMEM((CH, CH), BF16),
            dma((6,)), dma(()), dma((8,)), dma((2,)), dma((2,)),
        ] + [dma(())] * 5 + [dma((OWNERS,)), dma(()), dma(())],
        compiler_params=pltpu.CompilerParams(collective_id=0, has_side_effects=True, vmem_limit_bytes=40 * 2**20),
    )(*(
        pltpu.with_memory_space_constraint(array, pltpu.HBM)
        for array in (
            tokens.reshape(TOKENS, CH), cotangent.reshape(TOKENS, CH),
            qkv_weight, out_weight, cond_weight, head_scale,
        )
    ), timesteps)
    updated, grad = pl.pallas_call(
        hand_over,
        out_shape=(pltpu.HBM((TOKENS, CH), BF16), pltpu.HBM((CH, CH), F32)),
        in_specs=[pl.BlockSpec(memory_space=pl.ANY)] * 2,
        out_specs=(pl.BlockSpec(memory_space=pl.ANY),) * 2,
        scratch_shapes=[dma((2,))],
    )(pltpu.with_memory_space_constraint(updated, pltpu.VMEM), pltpu.with_memory_space_constraint(grad, pltpu.VMEM))
    return updated.reshape(tokens.shape), grad


def solution(mesh):
    return jax.shard_map(
        body,
        mesh=mesh,
        in_specs=(
            P("dp", "tile", None, None, None),
            P("dp"),
            P(),
            P(),
            P(),
            P(),
            P("dp", "tile", None, None, None),
        ),
        out_specs=(P("dp", "tile", None, None, None), P()),
        check_vma=False,
    )
```
